32 devices in a mesh: batch: 8 (over z, y), seq: 4 (over x, core).
Axes of the slice: x: 2, y: 2, z: 4, core: 2. Of those that a mesh axis runs over, the one named last changes fastest.
Arguments:
- inputs: bfloat16 [24, 1024, 512], P('batch', 'seq'), may hold values from -6 to 6
- counts: int32 [24], P('batch'), may hold values from 128 to 1024, as said below
- cotangent: bfloat16 [24, 1024, 512], P('batch', 'seq'), may hold values from -6 to 6
- attention_weights: float32 [4, 512, 512], P('seq', None, 'batch')
- attention_momenta: float32 [4, 512, 512], P('seq', None, 'batch')
- feed_weights: float32 [2, 512, 2048], P(None, None, ('batch', 'seq'))
- feed_momenta: float32 [2, 512, 2048], P(None, None, ('batch', 'seq'))
- vector_params: float32 [12, 512], P('seq', 'batch')
- vector_first: float32 [12, 512], P('seq', 'batch')
- vector_second: float32 [12, 512], P('seq', 'batch')
Outputs:
- layer_out: bfloat16 [24, 1024, 512], P('batch', 'seq')
- input_grad: bfloat16 [24, 1024, 512], P('batch', 'seq')
- attention_next: float32 [4, 512, 512], P('seq', None, 'batch')
- attention_moment: float32 [4, 512, 512], P('seq', None, 'batch')
- feed_next: float32 [2, 512, 2048], P(None, None, ('batch', 'seq'))
- feed_moment: float32 [2, 512, 2048], P(None, None, ('batch', 'seq'))
- vector_next: float32 [12, 512], P('seq', 'batch')
- vector_first_next: float32 [12, 512], P('seq', 'batch')
- vector_second_next: float32 [12, 512], P('seq', 'batch')
The draws below stay inside these ranges and needn't reach their ends.
Inputs may be any that keep to these rules, and one draw needn't show every extreme that they name: `counts`: in each aligned block of 3 sequences, one sequence has true tokens in the upper half of the slots of the last index of seq; some sequence has exactly 1024.
All inputs are finite; a program needn't handle non-finite values.
Results may differ from the reference program's by a relative error of at most 0.014.
Values may be sent and summed in bfloat16 or wider, within the bound.
No kernel may reach another device: no remote copies, remote signals or barrier semaphores. Data moves between devices by JAX's collectives and lax.ppermute only.
A program may use at most 128 MiB of HBM per device.

```python
from functools import partial
import jax
import jax.numpy as jnp
from jax import lax

D = 512
HEADS = 8
HEAD_DIM = 64
FF = 2048
LEN = 1024
SEQS = 3
STEP = 10
NS_STEPS = 5
ROWS = 24
TOKENS = 24576
N_SEQ = 4


def draw_counts(key, part):
    key = jax.random.fold_in(key, 7)
    length_key, long_key, slot_key, whole_key = jax.random.split(key, 4)
    groups = ROWS // SEQS
    lengths = jax.random.randint(length_key, (ROWS,), max(1, LEN // 8), LEN + 1)
    long_lengths = jax.random.randint(long_key, (groups,), LEN - LEN // (2 * N_SEQ) + 1, LEN + 1)
    long_slot = jax.random.randint(slot_key, (groups,), 0, SEQS)
    slot_index = jnp.arange(ROWS) % SEQS
    lengths = jnp.where(slot_index == jnp.repeat(long_slot, SEQS), jnp.repeat(long_lengths, SEQS), lengths)
    whole_group = jax.random.randint(whole_key, (), 0, groups)
    whole_row = whole_group * SEQS + long_slot[whole_group]
    lengths = jnp.where(jnp.arange(ROWS) == whole_row, LEN, lengths)
    return lengths.astype(jnp.int32)


def draw_attention_weights(key, part):
    key = jax.random.fold_in(key, 11)
    scales = jnp.array([1.0, 1.0, 1.0, 4.0], jnp.float32) * D ** (-0.5)
    base = jax.random.normal(key, (4, D, D), jnp.float32)
    return base * scales[:, None, None]


def draw_attention_momenta(key, part):
    key = jax.random.fold_in(key, 13)
    spread = 0.3 * TOKENS ** 0.5
    base = jax.random.normal(key, (4, D, D), jnp.float32)
    return base * spread


def draw_feed_weights(key, part):
    key = jax.random.fold_in(key, 17)
    scales = jnp.array([D ** (-0.5), FF ** (-0.5)], jnp.float32)
    base = jax.random.normal(key, (2, D, FF), jnp.float32)
    return base * scales[:, None, None]


def draw_feed_momenta(key, part):
    key = jax.random.fold_in(key, 19)
    spread = 0.2 * TOKENS ** 0.5
    base = jax.random.normal(key, (2, D, FF), jnp.float32)
    return base * spread


def draw_vector_params(key, part):
    key = jax.random.fold_in(key, 23)
    shift_key, gain_key = jax.random.split(key)
    shifts = 0.3 * jax.random.normal(shift_key, (12, D), jnp.float32)
    gains = 1.0 + jax.random.uniform(gain_key, (12, D), jnp.float32, -0.3, 0.3)
    row_index = jnp.arange(12)[:, None]
    is_gain = (row_index == 8) | (row_index == 10)
    return jnp.where(is_gain, gains, shifts)


def draw_vector_first(key, part):
    key = jax.random.fold_in(key, 29)
    spread = 0.05 * TOKENS ** 0.5
    base = jax.random.normal(key, (12, D), jnp.float32)
    return base * spread


def draw_vector_second(key, part):
    key = jax.random.fold_in(key, 31)
    lower = jnp.log(0.0003 * TOKENS)
    upper = jnp.log(0.004 * TOKENS)
    return jnp.exp(jax.random.uniform(key, (12, D), jnp.float32, lower, upper))


def steps_of(rng, extent, cuts, low, high):
    loudness, own = 1.0, jax.random.fold_in(rng, 6)
    for position, parts in cuts:
        draws = jnp.exp(jax.random.uniform(jax.random.fold_in(own, position), (parts,), jnp.float32, low / len(cuts), high / len(cuts)))
        loudness = loudness * jnp.repeat(draws, extent[position] // parts).reshape([-1 if axis == position else 1 for axis in range(len(extent))])
    return loudness


def bell_draw(stream_key, dims, width, most, shards=(), kind=jnp.bfloat16):
    factor_of = steps_of(stream_key, dims, shards, -0.22, 0.18) if shards else 1.0
    values = jax.random.normal(stream_key, dims, jnp.float32) * width * factor_of
    return jnp.minimum(jnp.maximum(values, -most), most).astype(kind)


def setup_inputs(seed: int = 0) -> dict:
    keys = jax.random.split(jax.random.key(seed), 11)
    inputs = bell_draw(keys[0], (ROWS, LEN, D), 1.0, 6.0, ((0, 8), (1, 4)))
    counts = draw_counts(jax.random.fold_in(keys[10], 71), 0)
    cotangent = bell_draw(keys[2], (ROWS, LEN, D), 1.0, 6.0, ((0, 8), (1, 4)))
    attention_weights = draw_attention_weights(jax.random.fold_in(keys[10], 71), 0)
    attention_momenta = draw_attention_momenta(jax.random.fold_in(keys[10], 71), 0)
    feed_weights = draw_feed_weights(jax.random.fold_in(keys[10], 71), 0)
    feed_momenta = draw_feed_momenta(jax.random.fold_in(keys[10], 71), 0)
    vector_params = draw_vector_params(jax.random.fold_in(keys[10], 71), 0)
    vector_first = draw_vector_first(jax.random.fold_in(keys[10], 71), 0)
    vector_second = draw_vector_second(jax.random.fold_in(keys[10], 71), 0)
    return {"inputs": inputs, "counts": counts, "cotangent": cotangent, "attention_weights": attention_weights, "attention_momenta": attention_momenta, "feed_weights": feed_weights, "feed_momenta": feed_momenta, "vector_params": vector_params, "vector_first": vector_first, "vector_second": vector_second}


newton_coef = (3.4445, -4.775, 2.0315)
muon_rate = 0.6
muon_decay = 0.95
adam_rate = 0.3
beta_one = 0.9
beta_two = 0.999
decay_rate = 0.01
adam_eps = 1e-08
norm_eps = 1e-05
masked_score = -1e+30
highest = lax.Precision.HIGHEST

@jax.custom_vjp
def low(v):
    return lax.optimization_barrier(v.astype(jnp.bfloat16)).astype(jnp.float32)

@jax.custom_vjp
def low_back(v):
    return v

def low_keep(v):
    return (low(v), None)

def low_pass(kept, grad):
    return (grad,)

def back_keep(v):
    return (v, None)

def back_low(kept, grad):
    return (low(grad),)
low.defvjp(low_keep, low_pass)
low_back.defvjp(back_keep, back_low)

def layer_norm(values_in, gain_vec, shift_vec):
    centre = values_in - lax.optimization_barrier(jnp.mean(values_in, axis=-1, keepdims=True))
    inverse_dev = lax.rsqrt(lax.optimization_barrier(jnp.mean(centre * centre, axis=-1, keepdims=True)) + norm_eps)
    return centre * inverse_dev * gain_vec + shift_vec

def smooth_gate(values_in):
    return jax.nn.gelu(values_in, approximate=True)

def matmul_high(left, right):
    return jnp.dot(left, right, precision=highest)

def attend_sequence(packed):
    query_rows, key_rows, value_rows, length = packed
    raw_scores = jnp.einsum('qhd,khd->hqk', query_rows, key_rows, precision=highest)
    scores = low_back(raw_scores * HEAD_DIM ** (-0.5))
    live_keys = jnp.arange(LEN) < length
    scores = jnp.where(live_keys[None, None, :], scores, masked_score)
    highest_score = lax.optimization_barrier(jnp.max(scores, axis=2, keepdims=True))
    exponents = jnp.exp(scores - highest_score)
    weights = low(exponents / lax.optimization_barrier(jnp.sum(exponents, axis=2, keepdims=True)))
    mixed = jnp.einsum('hqk,khd->qhd', weights, value_rows, precision=highest)
    return low(low_back(mixed)).reshape(LEN, HEADS * HEAD_DIM)

def layer(attention, feed, vectors, inputs_f, lengths):
    att_low = low(attention)
    feed_low = low(feed)
    vec_low = low(vectors)
    tokens = inputs_f.reshape(-1, D)
    queries = low(low_back(matmul_high(tokens, att_low[0]) + vec_low[0]))
    key_all = low(low_back(matmul_high(tokens, att_low[1])))
    value_all = low(low_back(matmul_high(tokens, att_low[2]) + vec_low[1]))
    group_size = inputs_f.shape[0]
    split_shape = (group_size, LEN, HEADS, HEAD_DIM)
    mixed = lax.map(jax.checkpoint(attend_sequence), (queries.reshape(split_shape), key_all.reshape(split_shape), value_all.reshape(split_shape), lengths))
    mixed = mixed.reshape(-1, D)
    attn_out = low_back(matmul_high(mixed, att_low[3]) + vec_low[2])
    normed = layer_norm(tokens + attn_out, vec_low[8], vec_low[9])
    up_pre = low_back(matmul_high(low(normed), feed_low[0]) + vec_low[3:7].reshape(FF))
    activated = low(smooth_gate(up_pre))
    down_out = low_back(matmul_high(activated, feed_low[1].T) + vec_low[7])
    summed = tokens + normed + down_out
    return layer_norm(summed, vec_low[10], vec_low[11]).reshape(inputs_f.shape)

def orthogonalize(moment):
    ortho = moment / (jnp.sqrt(jnp.sum(moment * moment)) + 1e-07)
    for iteration in range(NS_STEPS):
        square = matmul_high(ortho, ortho.T)
        poly = newton_coef[1] * square + newton_coef[2] * matmul_high(square, square)
        ortho = newton_coef[0] * ortho + matmul_high(poly, ortho)
    return ortho

def reference(inputs, counts, cotangent, attention_weights, attention_momenta, feed_weights, feed_momenta, vector_params, vector_first, vector_second):
    groups = ROWS // SEQS
    input_groups = inputs.astype(jnp.float32).reshape(groups, SEQS, LEN, D)
    length_groups = counts.reshape(groups, SEQS)
    cot_groups = cotangent.astype(jnp.float32).reshape(groups, SEQS, LEN, D)

    def one_group(running, packed):
        group_in, group_len, group_cot = packed
        group_out, pull_back = jax.vjp(partial(layer, lengths=group_len), attention_weights, feed_weights, vector_params, group_in)
        grad_att, grad_feed, grad_vec, grad_in = pull_back(group_cot)
        running = (running[0] + grad_att, running[1] + grad_feed, running[2] + grad_vec)
        return (running, (group_out.astype(jnp.bfloat16), grad_in.astype(jnp.bfloat16)))
    zero_grads = (jnp.zeros_like(attention_weights), jnp.zeros_like(feed_weights), jnp.zeros_like(vector_params))
    totals, results = lax.scan(one_group, zero_grads, (input_groups, length_groups, cot_groups))
    grad_att, grad_feed, grad_vec = totals
    layer_out = results[0].reshape(ROWS, LEN, D)
    input_grad = results[1].reshape(ROWS, LEN, D)
    attention_moment = muon_decay * attention_momenta + grad_att
    feed_moment = muon_decay * feed_momenta + grad_feed
    ortho_att = jnp.stack([orthogonalize(attention_moment[matrix_index]) for matrix_index in range(4)])
    ortho_feed = jnp.stack([orthogonalize(feed_moment[matrix_index]) for matrix_index in range(2)])
    attention_next = attention_weights * (1.0 - muon_rate * decay_rate) - muon_rate * ortho_att
    feed_next = feed_weights * (1.0 - muon_rate * decay_rate) - muon_rate * ortho_feed
    vector_first_next = beta_one * vector_first + (1.0 - beta_one) * grad_vec
    vector_second_next = beta_two * vector_second + (1.0 - beta_two) * grad_vec * grad_vec
    first_hat = vector_first_next / (1.0 - beta_one ** STEP)
    second_hat = vector_second_next / (1.0 - beta_two ** STEP)
    vector_next = vector_params * (1.0 - adam_rate * decay_rate) - adam_rate * first_hat / (jnp.sqrt(second_hat) + adam_eps)
    return (layer_out, input_grad, attention_next, attention_moment, feed_next, feed_moment, vector_next, vector_first_next, vector_second_next)
```

```python
import functools

import jax
import jax.numpy as jnp
from jax import lax
from jax.experimental import pallas as pl
from jax.experimental.pallas import tpu as pltpu
from jax.sharding import PartitionSpec as P

HEAD_DIM = 64
STEP = 10
NS_STEPS = 5

newton_coef = (3.4445, -4.775, 2.0315)
muon_rate = 0.6
muon_decay = 0.95
adam_rate = 0.3
beta_one = 0.9
beta_two = 0.999
decay_rate = 0.01
adam_eps = 1e-08
norm_eps = 1e-05
masked_score = -1e30
bf16 = jnp.bfloat16
f32 = jnp.float32
VMEM_LIMIT = 60 * 1024 * 1024

NN = (((1,), (0,)), ((), ()))
NT = (((1,), (1,)), ((), ()))
TN = (((0,), (0,)), ((), ()))


def dot(left, right, dims=NN):
    return lax.dot_general(left, right, dims, preferred_element_type=f32)


def xor_permute(value, axis, step):
    count = lax.axis_size(axis)
    return lax.ppermute(value, axis, [(i, i ^ step) for i in range(count)])


def halves(value):
    high = value.astype(bf16)
    return high, (value - high.astype(f32)).astype(bf16)


def dot_split(left, right, dims=NN):
    (left_high, left_low), (right_high, right_low) = left, right
    return (
        dot(left_high, right_high, dims)
        + dot(left_high, right_low, dims)
        + dot(left_low, right_high, dims)
    )


def newton_loop(square, rows):
    for turn in range(NS_STEPS):
        square_parts = halves(square)
        poly = newton_coef[1] * square + newton_coef[2] * dot_split(square_parts, square_parts)
        poly_parts = halves(poly)
        rows = newton_coef[0] * rows + dot_split(halves(rows), poly_parts)
        if turn + 1 < NS_STEPS:
            once = newton_coef[0] * square + dot_split(poly_parts, square_parts)
            square = newton_coef[0] * once + dot_split(halves(once), poly_parts)
    return rows


def newton_kernel(square_ref, rows_ref, out_ref):
    gram = square_ref[...]
    width = gram.shape[0]
    on_diagonal = lax.broadcasted_iota(jnp.int32, (width, width), 0) == lax.broadcasted_iota(
        jnp.int32, (width, width), 1
    )
    trace = jnp.sum(jnp.where(on_diagonal, gram, 0.0), keepdims=True)
    factor = 1.0 / (jnp.sqrt(trace) + 1e-07)
    out_ref[...] = newton_loop(gram * (factor * factor), rows_ref[...] * factor)


def gram_of_rows(rows):
    parts = halves(rows)
    return dot_split(parts, parts, TN)


def gram_kernel(rows_ref, out_ref):
    out_ref[...] = gram_of_rows(rows_ref[...])


def gram(rows):
    width = rows.shape[1]
    return pl.pallas_call(
        gram_kernel,
        out_shape=jax.ShapeDtypeStruct((width, width), f32),
        in_specs=[pl.BlockSpec(memory_space=pltpu.VMEM)],
        out_specs=pl.BlockSpec(memory_space=pltpu.VMEM),
        compiler_params=pltpu.CompilerParams(vmem_limit_bytes=VMEM_LIMIT),
        name="gram",
    )(rows)


def newton(gram, rows):
    return pl.pallas_call(
        newton_kernel,
        out_shape=jax.ShapeDtypeStruct(rows.shape, f32),
        in_specs=[pl.BlockSpec(memory_space=pltpu.VMEM)] * 2,
        out_specs=pl.BlockSpec(memory_space=pltpu.VMEM),
        compiler_params=pltpu.CompilerParams(vmem_limit_bytes=VMEM_LIMIT),
        name="newton",
    )(gram, rows)


def layer_norm(values_in, gain_vec, shift_vec):
    centre = values_in - jnp.mean(values_in, axis=-1, keepdims=True)
    inverse_dev = lax.rsqrt(jnp.mean(centre * centre, axis=-1, keepdims=True) + norm_eps)
    return centre * inverse_dev * gain_vec + shift_vec


def smooth_gate(values_in):
    return jax.nn.gelu(values_in, approximate=True)


def masked_scores(query_rows, key_rows, length):
    raw_scores = jnp.einsum("qhd,khd->hqk", query_rows, key_rows, preferred_element_type=f32)
    raw_scores = raw_scores * query_rows.shape[2] ** (-0.5)
    live_keys = jnp.arange(key_rows.shape[0]) < length
    return jnp.where(live_keys[None, None, :], raw_scores, masked_score)


def attend(query_rows, key_rows, value_rows, length):
    scores = masked_scores(query_rows, key_rows, length)
    highest_score = jnp.max(scores, axis=2, keepdims=True)
    exponents = jnp.exp(scores - highest_score)
    total_mass = jnp.sum(exponents, axis=2, keepdims=True)
    weights_low = (exponents / total_mass).astype(bf16)
    mixed = jnp.einsum("hqk,khd->qhd", weights_low, value_rows, preferred_element_type=f32)
    log_mass = (highest_score + jnp.log(total_mass))[:, :, 0]
    return (mixed.astype(bf16), log_mass)


def attend_back(query_rows, key_rows, value_rows, grad_mixed, log_mass, length):
    scores = masked_scores(query_rows, key_rows, length)
    weights = jnp.exp(scores - log_mass[:, :, None])
    grad_weights = jnp.einsum("qhd,khd->hqk", grad_mixed, value_rows, preferred_element_type=f32)
    inner_sum = jnp.sum(weights * grad_weights, axis=2, keepdims=True)
    grad_scores = (weights * (grad_weights - inner_sum)).astype(bf16)
    scale = query_rows.shape[2] ** (-0.5)
    grad_query = jnp.einsum("hqk,khd->qhd", grad_scores, key_rows, preferred_element_type=f32)
    grad_key = jnp.einsum("hqk,qhd->khd", grad_scores, query_rows, preferred_element_type=f32)
    grad_value = jnp.einsum(
        "hqk,qhd->khd", weights.astype(bf16), grad_mixed, preferred_element_type=f32
    )
    return (
        (grad_query * scale).astype(bf16),
        (grad_key * scale).astype(bf16),
        grad_value.astype(bf16),
    )


def weights_to_heads(payload, batch_index):
    batch_count, seq_count = lax.axis_size("batch"), lax.axis_size("seq")
    blocks = batch_count // seq_count
    pieces = []
    for turn in range(batch_count):
        route = []
        for block in range(batch_count):
            for member in range(seq_count):
                target = (member * blocks + block % blocks) ^ turn
                route.append(
                    (block * seq_count + member, target * seq_count + block // blocks)
                )
        pieces.append(lax.ppermute(payload, ("batch", "seq"), route))
    stacked = jnp.stack(pieces)
    return jnp.take(stacked, batch_index ^ jnp.arange(batch_count), axis=0)


def gather_relative(value, axis, order):
    pieces = [(0, value)]
    for step in order:
        pieces = pieces + [(offset ^ step, xor_permute(piece, axis, step)) for offset, piece in pieces]
    return pieces


def gather_direct(value, axis):
    count = lax.axis_size(axis)
    return [value] + [xor_permute(value, axis, step) for step in range(1, count)]


def natural(pieces, index):
    return jnp.take(jnp.stack(pieces), index ^ jnp.arange(len(pieces)), axis=0)


def sum_gram(part):
    low_count = 2
    width = part.shape[0]
    batch_count = lax.axis_size("batch")
    mine = lax.axis_index("seq") % low_count
    two = part.reshape(low_count, width // low_count, width)
    keep = lax.dynamic_index_in_dim(two, mine, 0, keepdims=False)
    send = lax.dynamic_index_in_dim(two, 1 - mine, 0, keepdims=False)
    half = keep + xor_permute(send, "seq", 1)
    rows = half.shape[0] // batch_count
    chunks = lax.all_to_all(
        half.reshape(batch_count, rows, width), "batch", split_axis=0, concat_axis=0, tiled=True
    )
    own = jnp.sum(chunks, axis=0)
    half = natural(gather_direct(own, "batch"), lax.axis_index("batch")).reshape(half.shape)
    other = xor_permute(half, "seq", 1)
    first = jnp.where(mine == 0, half, other)
    second = jnp.where(mine == 0, other, half)
    return jnp.concatenate([first, second], axis=0)


def shards(
    inputs,
    counts,
    cotangent,
    attention_weights,
    attention_momenta,
    feed_weights,
    feed_momenta,
    vector_params,
    vector_first,
    vector_second,
):
    seqs, local_len, width = inputs.shape
    seq_count, batch_count = lax.axis_size("seq"), lax.axis_size("batch")
    seq_index, batch_index = lax.axis_index("seq"), lax.axis_index("batch")
    full_len = local_len * seq_count
    tokens_count = seqs * local_len
    head_width = width // seq_count
    head_count = head_width // HEAD_DIM
    column_width = attention_weights.shape[2]
    feed_width = feed_weights.shape[2]
    hidden = feed_width * batch_count * seq_count
    vector_rows = vector_params.shape[0]

    att_own = attention_weights[0].T
    feed_own = feed_weights.transpose(0, 2, 1)
    moment_own = attention_momenta[0].T
    feed_moment_own = feed_momenta.transpose(0, 2, 1)
    vec_low = vector_params.astype(bf16)

    feed_all, vec_all = (
        lax.all_gather(feed_own.astype(bf16), ("seq", "batch"), axis=1, tiled=False),
        lax.all_gather(vec_low, ("seq", "batch"), axis=0, tiled=False),
    )
    moment_all = lax.all_gather(moment_own, "batch", axis=0, tiled=True)
    x_parts = gather_relative(inputs, "seq", [2, 1])
    x_parts = [piece for _, piece in sorted(x_parts, key=lambda pair: pair[0])]
    pad = jnp.zeros((16, width), bf16).at[0, : vector_rows * column_width].set(vec_low.reshape(-1))
    payload = jnp.concatenate([att_own.astype(bf16), pad], axis=0)
    head_parts = weights_to_heads(payload, batch_index)
    head_weights = head_parts[:, :column_width].reshape(seq_count, head_width, width)
    first_vecs = head_parts[: batch_count // seq_count, column_width, : vector_rows * column_width]
    first_vecs = first_vecs.reshape(-1, vector_rows, column_width).transpose(1, 0, 2)
    first_vecs = first_vecs.reshape(vector_rows, head_width).astype(f32)
    output_parts = gather_direct(head_weights[3], "seq")
    w_output_t = natural(output_parts, seq_index).reshape(width, width)
    vec_full = vec_all.reshape(seq_count, batch_count, vector_rows, column_width)
    vec_full = vec_full.transpose(0, 2, 1, 3).reshape(12, width).astype(f32)
    w_up_t = feed_all[0].reshape(hidden, width)
    w_down = feed_all[1].reshape(hidden, width)
    bias_up = vec_full[3:7].reshape(batch_count, seq_count, feed_width)
    bias_up = bias_up.transpose(1, 0, 2).reshape(hidden)
    bias_output, bias_down = vec_full[2], vec_full[7]
    gain_first, shift_first, gain_second, shift_second = (vec_full[row] for row in range(8, 12))

    upper = seq_count // 2
    matrix = seq_index // upper
    moment_send = lax.dynamic_index_in_dim(feed_moment_own, 1 - matrix, 0, keepdims=False)
    moment_keep = lax.dynamic_index_in_dim(feed_moment_own, matrix, 0, keepdims=False)
    moment_other = xor_permute(moment_send, "seq", upper)

    x_all = natural(x_parts, seq_index).transpose(1, 0, 2, 3).reshape(seqs, full_len, width)

    def project(part, bias):
        value = lax.dot_general(
            x_all, head_weights[part], (((2,), (1,)), ((), ())), preferred_element_type=f32
        )
        if bias is not None:
            value = value + bias
        return value.astype(bf16).reshape(seqs, full_len, head_count, HEAD_DIM)

    query = project(0, first_vecs[0])
    key = project(1, None)
    value = project(2, first_vecs[1])
    mixed_heads, log_mass = lax.map(lambda args: attend(*args), (query, key, value, counts))
    mixed_out = mixed_heads.reshape(seqs, seq_count, local_len, head_width).transpose(1, 0, 2, 3)
    mixed_tok = lax.all_to_all(mixed_out, "seq", split_axis=0, concat_axis=0, tiled=True)
    mixed_flat = mixed_tok.transpose(1, 2, 0, 3).reshape(tokens_count, width)

    tokens = inputs.reshape(tokens_count, width)
    attn_out = dot(mixed_flat, w_output_t, NT) + bias_output
    first_in = tokens.astype(f32) + attn_out
    normed, norm_first_back = jax.vjp(layer_norm, first_in, gain_first, shift_first)
    normed_low = normed.astype(bf16)
    up_pre = dot(normed_low, w_up_t, NT) + bias_up
    activated, gate_back = jax.vjp(smooth_gate, up_pre)
    activated_low = activated.astype(bf16)
    down_out = dot(activated_low, w_down) + bias_down
    summed = tokens.astype(f32) + normed + down_out
    result, norm_second_back = jax.vjp(layer_norm, summed, gain_second, shift_second)
    layer_out = result.astype(bf16).reshape(inputs.shape)
    grad_out = cotangent.reshape(tokens_count, width).astype(f32)
    grad_sum, grad_gain_second, grad_shift_second = norm_second_back(grad_out)
    grad_down_low = grad_sum.astype(bf16)
    grad_bias_down = jnp.sum(grad_down_low, axis=0, dtype=f32)
    grad_w_down = dot(activated_low, grad_down_low, TN).astype(bf16)
    grad_act = dot(grad_down_low, w_down, NT)
    grad_up_low = gate_back(grad_act)[0].astype(bf16)
    grad_bias_up = jnp.sum(grad_up_low, axis=0, dtype=f32)
    grad_w_up = dot(grad_up_low, normed_low, TN).astype(bf16)
    grad_normed = grad_sum + dot(grad_up_low, w_up_t)
    grad_first, grad_gain_first, grad_shift_first = norm_first_back(grad_normed)
    grad_attn_low = grad_first.astype(bf16)
    grad_bias_output = jnp.sum(grad_attn_low, axis=0, dtype=f32)
    grad_w_output = dot(grad_attn_low, mixed_flat, TN).astype(bf16)
    grad_mixed = dot(grad_attn_low, w_output_t).astype(bf16)
    grad_mixed = grad_mixed.reshape(seqs, local_len, seq_count, head_width).transpose(2, 0, 1, 3)
    grad_heads = lax.all_to_all(grad_mixed, "seq", split_axis=0, concat_axis=0, tiled=True)
    grad_heads = grad_heads.transpose(1, 0, 2, 3).reshape(seqs, full_len, head_count, HEAD_DIM)

    low_index = seq_index % upper
    feed_grads = jnp.stack([grad_w_up, grad_w_down])
    feed_grads = feed_grads.reshape(2, seq_count // upper, upper, -1, width)
    pair_keep = lax.dynamic_index_in_dim(feed_grads, low_index, 2, keepdims=False)
    pair_send = lax.dynamic_index_in_dim(feed_grads, low_index ^ 1, 2, keepdims=False)
    pair_sum = (pair_keep.astype(f32) + xor_permute(pair_send, "seq", 1).astype(f32)).astype(bf16)
    cross_keep = lax.dynamic_index_in_dim(pair_sum, matrix, 0, keepdims=False)
    cross_send = lax.dynamic_index_in_dim(pair_sum, 1 - matrix, 0, keepdims=False)
    cross_sum = cross_keep.astype(f32) + xor_permute(cross_send, "seq", upper).astype(f32)
    cross_sum = cross_sum.astype(bf16).reshape(2, batch_count, feed_width, width)
    feed_chunks = lax.all_to_all(
        cross_sum.transpose(1, 0, 2, 3), "batch", split_axis=0, concat_axis=0, tiled=True
    )
    feed_sum = jnp.sum(feed_chunks.astype(f32), axis=0)
    mine_first = matrix == 0
    moment_pair = jnp.where(
        mine_first, jnp.stack([moment_keep, moment_other]), jnp.stack([moment_other, moment_keep])
    )
    feed_moment_pair = muon_decay * moment_pair + feed_sum
    feed_rows = feed_moment_pair.reshape(2 * feed_width, width)
    gram_feed = sum_gram(gram(feed_rows))
    ortho_feed_pair = newton(gram_feed, feed_rows).reshape(2, feed_width, width)
    both_pair = jnp.stack([feed_moment_pair, ortho_feed_pair], axis=1)
    both_keep = lax.dynamic_index_in_dim(both_pair, matrix, 0, keepdims=False)
    both_send = lax.dynamic_index_in_dim(both_pair, 1 - matrix, 0, keepdims=False)
    both_other = xor_permute(both_send, "seq", upper)
    both = jnp.where(
        mine_first, jnp.stack([both_keep, both_other], 1), jnp.stack([both_other, both_keep], 1)
    )
    feed_moment = both[0].transpose(0, 2, 1)
    ortho_feed = both[1].transpose(0, 2, 1)

    grad_query, grad_key, grad_value = lax.map(
        lambda args: attend_back(*args), (query, key, value, grad_heads, log_mass, counts)
    )
    flat_x = x_all.reshape(-1, width)
    head_grads = [
        grad.reshape(-1, head_width) for grad in (grad_query, grad_key, grad_value)
    ]
    head_weight_grads = [dot(grad, flat_x, TN).astype(bf16) for grad in head_grads]
    back_part = sum(dot(grad, head_weights[i]) for i, grad in enumerate(head_grads))
    back_part = back_part.astype(bf16).reshape(seqs, seq_count, local_len, width)
    back_part = jnp.take(back_part, seq_index ^ jnp.arange(seq_count), axis=1)
    low_half = [back_part[:, 0].astype(f32), back_part[:, upper].astype(f32)]
    low_got = xor_permute(
        jnp.stack([back_part[:, 1], back_part[:, upper + 1]]), "seq", 1
    ).astype(f32)
    high_got = xor_permute((low_half[1] + low_got[1]).astype(bf16), "seq", upper).astype(f32)
    grad_tokens = (grad_sum + grad_first).reshape(inputs.shape)
    input_grad = (grad_tokens + low_half[0] + low_got[0] + high_got).astype(bf16)

    output_chunks = lax.all_to_all(
        grad_w_output.reshape(seq_count, head_width, width),
        "seq",
        split_axis=0,
        concat_axis=0,
        tiled=True,
    )
    output_sum = jnp.sum(output_chunks.astype(f32), axis=0).astype(bf16)
    att_grads = jnp.stack(head_weight_grads + [output_sum])
    att_grads = att_grads.reshape(seq_count, batch_count, -1, 128).transpose(1, 0, 2, 3)

    def at_heads(grad):
        return lax.dynamic_update_slice(
            jnp.zeros((width,), f32), jnp.sum(grad, axis=0, dtype=f32), (seq_index * head_width,)
        )

    vec_grads = jnp.concatenate(
        [
            jnp.stack([at_heads(head_grads[0]), at_heads(head_grads[2]), grad_bias_output]),
            grad_bias_up.reshape(seq_count, batch_count, feed_width)
            .transpose(1, 0, 2)
            .reshape(4, width),
            jnp.stack(
                [
                    grad_bias_down,
                    grad_gain_first,
                    grad_shift_first,
                    grad_gain_second,
                    grad_shift_second,
                ]
            ),
        ]
    )
    vec_grads = vec_grads.astype(bf16).reshape(seq_count, vector_rows, batch_count, column_width)
    vec_grads = vec_grads.transpose(2, 0, 1, 3).reshape(batch_count, seq_count, -1)
    vec_grads = jnp.pad(vec_grads, ((0, 0), (0, 0), (0, 2048 - vec_grads.shape[2])))
    vec_grads = vec_grads.reshape(batch_count, seq_count, 16, 128)
    att_rows = att_grads.shape[2]
    payload = jnp.concatenate([att_grads, vec_grads], axis=2)
    payload = payload.reshape(batch_count * seq_count, att_rows + 16, 128)
    got = lax.all_to_all(payload, ("batch", "seq"), split_axis=0, concat_axis=0, tiled=True)
    got = got.reshape(batch_count, seq_count, att_rows + 16, 128).astype(f32)
    att_sum = jnp.sum(got[:, :, :att_rows], axis=0).astype(bf16)
    grad_vec = jnp.sum(got[:, :, att_rows:], axis=(0, 1)).reshape(-1)
    grad_vec = grad_vec[: vector_rows * column_width].reshape(vector_rows, column_width)
    att_full = natural(gather_direct(att_sum, "batch"), batch_index)
    att_full = att_full.transpose(1, 0, 2, 3).reshape(width, width)
    att_rows_all = muon_decay * moment_all + att_full.astype(f32)
    gram_att = gram(att_rows_all)
    att_rows_own = lax.dynamic_slice_in_dim(att_rows_all, batch_index * column_width, column_width)
    ortho_att = newton(gram_att, att_rows_own).T[None]
    attention_moment = att_rows_own.T[None]

    attention_next = attention_weights * (1.0 - muon_rate * decay_rate) - muon_rate * ortho_att
    feed_next = feed_weights * (1.0 - muon_rate * decay_rate) - muon_rate * ortho_feed
    vector_first_next = beta_one * vector_first + (1.0 - beta_one) * grad_vec
    vector_second_next = beta_two * vector_second + (1.0 - beta_two) * grad_vec * grad_vec
    first_hat = vector_first_next / (1.0 - beta_one**STEP)
    second_hat = vector_second_next / (1.0 - beta_two**STEP)
    vector_next = vector_params * (1.0 - adam_rate * decay_rate) - adam_rate * first_hat / (
        jnp.sqrt(second_hat) + adam_eps
    )
    return (
        layer_out,
        input_grad,
        attention_next,
        attention_moment,
        feed_next,
        feed_moment,
        vector_next,
        vector_first_next,
        vector_second_next,
    )


def solution(mesh):
    tokens_spec = P("batch", "seq", None)
    attention_spec = P("seq", None, "batch")
    feed_spec = P(None, None, ("batch", "seq"))
    vector_spec = P("seq", "batch")
    return jax.shard_map(
        shards,
        mesh=mesh,
        in_specs=(tokens_spec, P("batch"), tokens_spec)
        + (attention_spec,) * 2
        + (feed_spec,) * 2
        + (vector_spec,) * 3,
        out_specs=(tokens_spec,) * 2
        + (attention_spec,) * 2
        + (feed_spec,) * 2
        + (vector_spec,) * 3,
        check_vma=False,
    )
```

```python
import functools

import jax
import jax.numpy as jnp
from jax import lax
from jax.experimental import pallas as pl
from jax.experimental.pallas import tpu as pltpu
from jax.sharding import PartitionSpec as P

HEAD_DIM = 64
STEP = 10
NS_STEPS = 5

newton_coef = (3.4445, -4.775, 2.0315)
muon_rate = 0.6
muon_decay = 0.95
adam_rate = 0.3
beta_one = 0.9
beta_two = 0.999
decay_rate = 0.01
adam_eps = 1e-08
norm_eps = 1e-05
masked_score = -1e30
bf16 = jnp.bfloat16
f32 = jnp.float32
VMEM_LIMIT = 60 * 1024 * 1024


def cost(micros):
    return pl.CostEstimate(flops=int(micros * 1.15e9), bytes_accessed=1 << 20, transcendentals=0)

NN = (((1,), (0,)), ((), ()))
NT = (((1,), (1,)), ((), ()))
TN = (((0,), (0,)), ((), ()))


def dot(left, right, dims=NN):
    return lax.dot_general(left, right, dims, preferred_element_type=f32)


def xor_permute(value, axis, step):
    count = lax.axis_size(axis)
    return lax.ppermute(value, axis, [(i, i ^ step) for i in range(count)])


def halves(value):
    high = value.astype(bf16)
    return high, (value - high.astype(f32)).astype(bf16)


def dot_split(left, right, dims=NN):
    (left_high, left_low), (right_high, right_low) = left, right
    return (
        dot(left_high, right_high, dims)
        + dot(left_high, right_low, dims)
        + dot(left_low, right_high, dims)
    )


def newton_loop(square, rows):
    for turn in range(NS_STEPS):
        square_parts = halves(square)
        poly = newton_coef[1] * square + newton_coef[2] * dot_split(square_parts, square_parts)
        poly_parts = halves(poly)
        rows = newton_coef[0] * rows + dot_split(halves(rows), poly_parts)
        if turn + 1 < NS_STEPS:
            once = newton_coef[0] * square + dot_split(poly_parts, square_parts)
            square = newton_coef[0] * once + dot_split(halves(once), poly_parts)
    return rows


def newton_kernel(square_ref, rows_ref, out_ref):
    gram = square_ref[...]
    width = gram.shape[0]
    on_diagonal = lax.broadcasted_iota(jnp.int32, (width, width), 0) == lax.broadcasted_iota(
        jnp.int32, (width, width), 1
    )
    trace = jnp.sum(jnp.where(on_diagonal, gram, 0.0), keepdims=True)
    factor = 1.0 / (jnp.sqrt(trace) + 1e-07)
    out_ref[...] = newton_loop(gram * (factor * factor), rows_ref[...] * factor)


def gram_of_rows(rows):
    parts = halves(rows)
    return dot_split(parts, parts, TN)


def normalized(gram, rows):
    width = gram.shape[0]
    shape = (width, width)
    on_diagonal = lax.broadcasted_iota(jnp.int32, shape, 0) == lax.broadcasted_iota(
        jnp.int32, shape, 1
    )
    trace = jnp.sum(jnp.where(on_diagonal, gram, 0.0), keepdims=True)
    factor = 1.0 / (jnp.sqrt(trace) + 1e-07)
    return gram * (factor * factor), rows * factor


def gram_kernel(rows_ref, out_ref):
    out_ref[...] = gram_of_rows(rows_ref[...])


def gram(rows):
    width = rows.shape[1]
    return pl.pallas_call(
        gram_kernel,
        out_shape=jax.ShapeDtypeStruct((width, width), f32),
        in_specs=[pl.BlockSpec(memory_space=pltpu.VMEM)],
        out_specs=pl.BlockSpec(memory_space=pltpu.VMEM),
        compiler_params=pltpu.CompilerParams(vmem_limit_bytes=VMEM_LIMIT),
        cost_estimate=cost(2),
        name="gram",
    )(rows)


def newton_kernel(index_ref, half_ref, other_ref, rows_ref, out_ref, square_ref):
    size = half_ref.shape[0]
    for distance, part_ref in enumerate((half_ref, other_ref)):
        start = pl.multiple_of(((index_ref[0] % 2) ^ distance) * size, size)
        square_ref[pl.ds(start, size), :] = part_ref[...]
    out_ref[...] = newton_loop(*normalized(square_ref[...], rows_ref[...]))


def newton(info, half, other, rows):
    width = rows.shape[1]
    return pl.pallas_call(
        newton_kernel,
        out_shape=jax.ShapeDtypeStruct(rows.shape, f32),
        in_specs=[pl.BlockSpec(memory_space=pltpu.SMEM)]
        + [pl.BlockSpec(memory_space=pltpu.VMEM)] * 3,
        out_specs=pl.BlockSpec(memory_space=pltpu.VMEM),
        scratch_shapes=[pltpu.VMEM((width, width), f32)],
        compiler_params=pltpu.CompilerParams(vmem_limit_bytes=VMEM_LIMIT),
        cost_estimate=cost(15),
        name="newton",
    )(info, half, other, rows)


def newton_whole_kernel(index_ref, *refs, count):
    pieces, (old_ref, _, moment_ref, out_ref, rows_ref) = refs[:count], refs[count:]
    own = moment_ref.shape[0]
    members, step = pieces[0].shape[:2]
    stride = rows_ref.shape[0] // members
    for turn in range(count):
        place = (index_ref[0] ^ turn) * step if count > 1 else 0
        for member in range(members):
            rows = pl.ds(member * stride + pl.multiple_of(place, 8), step)
            rows_ref[rows, :] = muon_decay * old_ref[rows, :] + pieces[turn][member].astype(f32)
    gram = gram_of_rows(rows_ref[...])
    rows = rows_ref[pl.ds(pl.multiple_of(index_ref[0] * own, 8), own), :]
    moment_ref[...] = rows
    out_ref[...] = newton_loop(*normalized(gram, rows))


def newton_whole(index, pieces, old, own, after):
    if pieces[0].shape[1] % 8:
        pieces = [natural(pieces, index).transpose(1, 0, 2, 3).reshape(1, *old.shape)]
    shape = jax.ShapeDtypeStruct((own, old.shape[1]), f32)
    return pl.pallas_call(
        functools.partial(newton_whole_kernel, count=len(pieces)),
        out_shape=(shape, shape),
        in_specs=[pl.BlockSpec(memory_space=pltpu.SMEM)]
        + [pl.BlockSpec(memory_space=pltpu.VMEM)] * (len(pieces) + 1)
        + [pl.BlockSpec(memory_space=pl.ANY)],
        out_specs=(pl.BlockSpec(memory_space=pltpu.VMEM),) * 2,
        scratch_shapes=[pltpu.VMEM(old.shape, f32)],
        compiler_params=pltpu.CompilerParams(vmem_limit_bytes=VMEM_LIMIT),
        cost_estimate=cost(17),
        name="newton_whole",
    )(index[None].astype(jnp.int32), *pieces, old, after)


def norm_parts(values_in):
    centre = values_in - jnp.mean(values_in, axis=-1, keepdims=True)
    inverse_dev = lax.rsqrt(jnp.mean(centre * centre, axis=-1, keepdims=True) + norm_eps)
    return centre * inverse_dev, inverse_dev


def norm_back(grad, normal, inverse_dev, gain):
    scaled = grad * gain
    mean_scaled = jnp.mean(scaled, axis=-1, keepdims=True)
    mean_normal = jnp.mean(scaled * normal, axis=-1, keepdims=True)
    return inverse_dev * (scaled - mean_scaled - normal * mean_normal)


def column_sum(values_in):
    return jnp.sum(values_in.astype(f32), axis=0, keepdims=True)


def token_kernel(info_ref, x_ref, cotangent_ref, feed_ref, vec_ref, up_bias_ref, *refs, ranges):
    seqs, block, width = x_ref.shape
    mixed_refs, refs = refs[: len(ranges)], refs[len(ranges) :]
    seq_count = mixed_refs[0].shape[0]
    output_refs, refs = refs[:seq_count], refs[seq_count:]
    grad_mixed_ref, refs = refs[0], refs[1:]
    out_ref, gate_ref, up_grad_ref, normed_ref, down_grad_ref = refs[:5]
    attn_grad_ref, mixed_flat_ref, rest_ref, sums_ref, up_sums_ref = refs[5:10]
    w_output_ref, slope_ref = refs[10:]
    tokens = seqs * block
    head_width = width // seq_count
    pieces, feed_width = feed_ref.shape[0], (feed_ref.shape[1] - 16) // 2
    chunk_pieces = max(1, pieces // 4)
    chunk = chunk_pieces * feed_width
    chunks = pieces // chunk_pieces

    def weights(matrix, i):
        rows = slice(matrix * feed_width, (matrix + 1) * feed_width)
        return feed_ref[i * chunk_pieces : (i + 1) * chunk_pieces, rows].reshape(chunk, width)

    def vec(row):
        return vec_ref[row : row + 1]

    for offset in range(seq_count):
        start = pl.multiple_of((info_ref[0] ^ offset) * head_width, head_width)
        w_output_ref[pl.ds(start, head_width), :] = output_refs[offset][...]
    for place in range(seq_count):
        lanes = slice(place * head_width, (place + 1) * head_width)
        for mixed_ref, (first, count) in zip(mixed_refs, ranges):
            rows = slice(first * block, (first + count) * block)
            mixed_flat_ref[rows, lanes] = mixed_ref[place].reshape(count * block, head_width)
    x = x_ref[...].reshape(tokens, width).astype(f32)
    attn_out = dot(mixed_flat_ref[...], w_output_ref[...], NT) + vec(2)
    normal_first, inverse_first = norm_parts(x + attn_out)
    normed = normal_first * vec(8) + vec(9)
    normed_low = normed.astype(bf16)
    normed_ref[...] = normed_low
    down_out = vec(7)
    curve, cubic = (2.0 / jnp.pi) ** 0.5, 0.044715
    for i in range(chunks):
        lanes = slice(i * chunk, (i + 1) * chunk)
        up = dot(normed_low, weights(0, i), NT) + up_bias_ref[:, lanes]
        square = up * up
        bend = jnp.tanh(up * (curve + (curve * cubic) * square))
        half = 0.5 + 0.5 * bend
        gate = (up * half).astype(bf16)
        gate_ref[:, lanes] = gate
        slope_ref[:, lanes] = half + (0.5 * up) * (1.0 - bend * bend) * (
            curve + (3.0 * curve * cubic) * square
        )
        down_out = down_out + dot(gate, weights(1, i))
    normal_second, inverse_second = norm_parts(x + normed + down_out)
    out = normal_second * vec(10) + vec(11)
    out_ref[...] = out.astype(bf16).reshape(out_ref.shape)
    grad_out = cotangent_ref[...].reshape(tokens, width).astype(f32)
    grad_sum = norm_back(grad_out, normal_second, inverse_second, vec(10))
    sums_ref[4:5] = column_sum(grad_out * normal_second)
    sums_ref[5:6] = column_sum(grad_out)
    grad_down_low = grad_sum.astype(bf16)
    down_grad_ref[...] = grad_down_low
    sums_ref[1:2] = column_sum(grad_down_low)
    grad_normed = grad_sum
    for i in range(chunks):
        lanes = slice(i * chunk, (i + 1) * chunk)
        grad_up = dot(grad_down_low, weights(1, i), NT) * slope_ref[:, lanes]
        grad_up_low = grad_up.astype(bf16)
        up_grad_ref[:, lanes] = grad_up_low
        up_sums_ref[0:1, lanes] = column_sum(grad_up_low)
        grad_normed = grad_normed + dot(grad_up_low, weights(0, i))
    grad_first = norm_back(grad_normed, normal_first, inverse_first, vec(8))
    sums_ref[2:3] = column_sum(grad_normed * normal_first)
    sums_ref[3:4] = column_sum(grad_normed)
    grad_attn_low = grad_first.astype(bf16)
    attn_grad_ref[...] = grad_attn_low
    sums_ref[0:1] = column_sum(grad_attn_low)
    rest_ref[...] = grad_sum + grad_first
    grad_mixed = dot(grad_attn_low, w_output_ref[...]).astype(bf16)
    for place in range(seq_count):
        lanes = slice(place * head_width, (place + 1) * head_width)
        grad_mixed_ref[place] = grad_mixed[:, lanes].reshape(seqs, block, head_width)


def token_part(info, x, mixed, cotangent, feed_all, vec_full, up_bias, output_parts, ranges):
    seqs, block, width = x.shape
    tokens = seqs * block
    if (feed_all.shape[1] - 16) // 2 % 16:
        rows = (feed_all.shape[1] - 16) // 2
        parts = [feed_all[:, i * rows : (i + 1) * rows].reshape(-1, width) for i in range(2)]
        feed_all = jnp.concatenate(parts + [jnp.zeros((16, width), bf16)])[None]
    hidden = up_bias.shape[1]

    def shape(*dims, kind=bf16):
        return jax.ShapeDtypeStruct(dims, kind)

    vmem = pl.BlockSpec(memory_space=pltpu.VMEM)
    return pl.pallas_call(
        functools.partial(token_kernel, ranges=ranges),
        out_shape=(
            shape(mixed[0].shape[0], seqs, block, mixed[0].shape[3]),
            shape(seqs, block, width),
            shape(tokens, hidden),
            shape(tokens, hidden),
            shape(tokens, width),
            shape(tokens, width),
            shape(tokens, width),
            shape(tokens, width),
            shape(tokens, width, kind=f32),
            shape(8, width, kind=f32),
            shape(8, hidden, kind=f32),
        ),
        in_specs=[pl.BlockSpec(memory_space=pltpu.SMEM)] + [vmem] * (5 + len(mixed) + len(output_parts)),
        out_specs=(vmem,) * 11,
        scratch_shapes=[pltpu.VMEM((width, width), bf16), pltpu.VMEM((tokens, hidden), f32)],
        compiler_params=pltpu.CompilerParams(vmem_limit_bytes=VMEM_LIMIT),
        cost_estimate=cost(17),
        name="token_part",
    )(info, x, cotangent, feed_all, vec_full, up_bias, *mixed, *output_parts)


def feed_grad_kernel(info_ref, gate_ref, grad_up_ref, normed_ref, grad_down_ref, *refs):
    upper, rows = refs[0].shape[1:3]
    for distance, out_ref in enumerate(refs):
        for part in range(upper):
            block = part * 2 + ((info_ref[0] % 2) ^ distance)
            lanes = pl.ds(pl.multiple_of(block * rows, rows), rows)
            made = dot(grad_up_ref[:, lanes], normed_ref[...], TN)
            out_ref[0, part] = made.astype(bf16)
            made = dot(gate_ref[:, lanes], grad_down_ref[...], TN)
            out_ref[1, part] = made.astype(bf16)


def feed_grads(info, gate, grad_up, normed, grad_down, seq_count):
    hidden, width = gate.shape[1], normed.shape[1]
    shape = jax.ShapeDtypeStruct((2, seq_count // 2, hidden // seq_count, width), bf16)
    vmem = pl.BlockSpec(memory_space=pltpu.VMEM)
    return pl.pallas_call(
        feed_grad_kernel,
        out_shape=(shape, shape),
        in_specs=[pl.BlockSpec(memory_space=pltpu.SMEM)] + [vmem] * 4,
        out_specs=(vmem, vmem),
        compiler_params=pltpu.CompilerParams(vmem_limit_bytes=VMEM_LIMIT),
        cost_estimate=cost(1),
        name="feed_grads",
    )(info, gate, grad_up, normed, grad_down)


LOG2_E = 1.4426950408889634


def attend_kernel(info_ref, *refs, piece_count, head_width, first):
    x_refs, weight_ref = refs[:piece_count], refs[piece_count]
    query_ref, key_ref, value_ref, mixed_ref, mass_ref = refs[-5:]
    seq_index, length = info_ref[0], info_ref[1 + first + pl.program_id(0)]
    block = x_refs[0].shape[1]
    own_lanes = pl.ds(pl.multiple_of(seq_index * head_width, head_width), head_width)
    vecs = weight_ref[0, head_width:, own_lanes].astype(f32)
    biases = (vecs[0:1], vecs[1:2])
    for offset in range(piece_count):
        rows = pl.ds(pl.multiple_of((seq_index ^ offset) * block, block), block)
        for member, made_ref in enumerate((query_ref, key_ref, value_ref)):
            made = dot(x_refs[offset][0], weight_ref[member, :head_width], NT)
            if member != 1:
                made = made + biases[member // 2]
            made_ref[0, rows, :] = made.astype(bf16)
    factor = HEAD_DIM**-0.5 * LOG2_E
    live_blocks = (length + block - 1) // block

    def attend_blocks(count):
        key_rows = lax.broadcasted_iota(jnp.int32, (block, block), 0) + (count - 1) * block
        live = key_rows < length

        @pl.loop(0, piece_count)
        def _(place):
            rows = pl.ds(pl.multiple_of(place * block, block), block)
            outs = []
            for head in range(head_width // HEAD_DIM):
                lanes = slice(head * HEAD_DIM, (head + 1) * HEAD_DIM)
                query = query_ref[0, rows, lanes]
                tiles = []
                top = None
                for i in range(count):
                    tile = dot(key_ref[0, i * block : (i + 1) * block, lanes], query, NT)
                    if i == count - 1:
                        tile = jnp.where(live, tile, masked_score)
                    tiles.append(tile)
                    tile_top = jnp.max(tile, axis=0, keepdims=True)
                    top = tile_top if top is None else jnp.maximum(top, tile_top)
                top = top * factor
                mass, mixed = None, None
                for i in range(count):
                    tile = jnp.exp2(tiles[i] * factor - top)
                    tile_mass = jnp.sum(tile, axis=0, keepdims=True)
                    mass = tile_mass if mass is None else mass + tile_mass
                    value = value_ref[0, i * block : (i + 1) * block, lanes]
                    tile_mixed = dot(value, tile.astype(bf16), TN)
                    mixed = tile_mixed if mixed is None else mixed + tile_mixed
                outs.append(mixed / mass)
                mass_ref[0, head : head + 1, rows] = top + jnp.log2(mass)
            mixed_ref[place, 0] = jnp.concatenate(outs, axis=0).T.astype(bf16)

    for count in range(1, piece_count + 1):
        pl.when(live_blocks == count)(functools.partial(attend_blocks, count))


def attend(info, x_parts, weight, first, seqs, after):
    piece_count = len(x_parts)
    _, block, width = x_parts[0].shape
    head_width = width // piece_count
    full_len = piece_count * block
    heads_shape = jax.ShapeDtypeStruct((seqs, full_len, head_width), bf16)
    heads_spec = pl.BlockSpec((1, full_len, head_width), lambda i, _: (i, 0, 0))
    return pl.pallas_call(
        functools.partial(
            attend_kernel, piece_count=piece_count, head_width=head_width, first=first
        ),
        out_shape=(heads_shape,) * 3
        + (
            jax.ShapeDtypeStruct((piece_count, seqs, block, head_width), bf16),
            jax.ShapeDtypeStruct((seqs, 8, full_len), f32),
        ),
        grid_spec=pltpu.PrefetchScalarGridSpec(
            num_scalar_prefetch=1,
            grid=(seqs,),
            in_specs=[pl.BlockSpec((1, block, width), lambda i, _: (first + i, 0, 0))] * piece_count
            + [pl.BlockSpec(weight.shape, lambda i, _: (0, 0, 0))]
            + [pl.BlockSpec(memory_space=pl.ANY)] * len(after),
            out_specs=(heads_spec,) * 3
            + (
                pl.BlockSpec((piece_count, 1, block, head_width), lambda i, _: (0, i, 0, 0)),
                pl.BlockSpec((1, 8, full_len), lambda i, _: (i, 0, 0)),
            ),
        ),
        compiler_params=pltpu.CompilerParams(vmem_limit_bytes=VMEM_LIMIT),
        cost_estimate=cost(7 * seqs),
        name="attend",
    )(info, *x_parts, weight, *after)


def attend_back_kernel(info_ref, *refs, piece_count, head_width, first, sum_count, after_count):
    x_refs, refs = refs[:piece_count], refs[piece_count:]
    weight_ref, query_ref, key_ref, value_ref, mixed_ref, grad_ref, mass_ref = refs[:7]
    sum_refs, refs = refs[7 : 7 + sum_count], refs[7 + sum_count + after_count :]
    back_ref, weight_grad_ref, bias_grad_ref, query_acc, key_acc, value_acc = refs
    step = pl.program_id(0)
    seq_index, length = info_ref[0], info_ref[1 + first + step]
    block = x_refs[0].shape[1]
    full_len = block * piece_count
    factor = HEAD_DIM**-0.5 * LOG2_E
    scale = HEAD_DIM**-0.5
    live_blocks = (length + block - 1) // block
    heads = head_width // HEAD_DIM
    query_acc[...] = jnp.zeros_like(query_acc)

    inner = []
    head_of_lane = lax.broadcasted_iota(jnp.int32, (8, head_width), 1) // HEAD_DIM
    picks = (head_of_lane == lax.broadcasted_iota(jnp.int32, (8, head_width), 0)).astype(bf16)
    for place in range(piece_count):
        product = mixed_ref[place, 0].astype(f32) * grad_ref[place, 0].astype(f32)
        high, low = halves(product)
        inner.append(dot(picks, high, NT) + dot(picks, low, NT))

    @pl.loop(0, live_blocks)
    def _(k):
        rows = pl.ds(pl.multiple_of(k * block, block), block)
        live = lax.broadcasted_iota(jnp.int32, (block, block), 0) + k * block < length
        key_out, value_out = [], []
        for head in range(heads):
            lanes = slice(head * HEAD_DIM, (head + 1) * HEAD_DIM)
            key, value = key_ref[0, rows, lanes], value_ref[0, rows, lanes]
            key_grad, value_grad = None, None
            for place in range(piece_count):
                columns = slice(place * block, (place + 1) * block)
                query = query_ref[0, columns, lanes]
                grad = grad_ref[place, 0, :, lanes]
                tile = dot(key, query, NT) * factor - mass_ref[0, head : head + 1, columns]
                weights = jnp.exp2(jnp.where(live, tile, masked_score))
                tile = dot(value, grad, NT) - inner[place][head : head + 1]
                score_grad = (weights * tile).astype(bf16)
                part = dot(weights.astype(bf16), grad)
                value_grad = part if value_grad is None else value_grad + part
                part = dot(score_grad, query)
                key_grad = part if key_grad is None else key_grad + part
                query_acc[lanes, columns] += dot(key, score_grad, TN)
            key_out.append(key_grad * scale)
            value_out.append(value_grad)
        key_acc[rows, :] = jnp.concatenate(key_out, axis=1).astype(bf16)
        value_acc[rows, :] = jnp.concatenate(value_out, axis=1).astype(bf16)

    @pl.loop(live_blocks, piece_count)
    def _(k):
        rows = pl.ds(pl.multiple_of(k * block, block), block)
        key_acc[rows, :] = jnp.zeros((block, head_width), bf16)
        value_acc[rows, :] = jnp.zeros((block, head_width), bf16)

    @pl.when(step == 0)
    def _():
        if sum_refs:
            weight_grad_ref[...] = sum_refs[0][...]
            bias_grad_ref[...] = sum_refs[1][...]
        else:
            weight_grad_ref[...] = jnp.zeros_like(weight_grad_ref)
            bias_grad_ref[...] = jnp.zeros_like(bias_grad_ref)

    ones = jnp.ones((8, block), bf16)
    for offset in range(piece_count):
        start = pl.multiple_of((seq_index ^ offset) * block, block)
        rows = pl.ds(start, block)
        query_grad_t = (query_acc[:, rows] * scale).astype(bf16)
        query_grad = query_grad_t.T
        key_grad, value_grad = key_acc[rows, :], value_acc[rows, :]
        x = x_refs[offset][0]
        weight_grad_ref[:head_width] += dot(query_grad_t, x)
        weight_grad_ref[head_width : 2 * head_width] += dot(key_grad, x, TN)
        weight_grad_ref[2 * head_width :] += dot(value_grad, x, TN)
        bias_grad_ref[0] += dot(ones, query_grad)
        bias_grad_ref[1] += dot(ones, value_grad)
        back = dot(query_grad, weight_ref[0, :head_width])
        back = back + dot(key_grad, weight_ref[1, :head_width])
        back = back + dot(value_grad, weight_ref[2, :head_width])
        back_ref[offset, 0] = back.astype(bf16)


def attend_back(info, x_parts, weight, saved, grad, first, place, sums, after):
    piece_count = len(x_parts)
    _, block, width = x_parts[0].shape
    head_width = width // piece_count
    full_len = piece_count * block
    query, key, value, mixed, mass = saved
    seqs = 1
    heads_spec = pl.BlockSpec((1, full_len, head_width), lambda i, _: (place + i, 0, 0))

    def pieces_spec(row):
        return pl.BlockSpec((piece_count, 1, block, head_width), lambda i, _: (0, row + i, 0, 0))

    return pl.pallas_call(
        functools.partial(
            attend_back_kernel,
            piece_count=piece_count,
            head_width=head_width,
            first=first,
            sum_count=len(sums),
            after_count=len(after),
        ),
        out_shape=(
            jax.ShapeDtypeStruct((piece_count, seqs, block, width), bf16),
            jax.ShapeDtypeStruct((3 * head_width, width), f32),
            jax.ShapeDtypeStruct((2, 8, head_width), f32),
        ),
        grid_spec=pltpu.PrefetchScalarGridSpec(
            num_scalar_prefetch=1,
            grid=(seqs,),
            in_specs=[pl.BlockSpec((1, block, width), lambda i, _: (first + i, 0, 0))] * piece_count
            + [pl.BlockSpec(weight.shape, lambda i, _: (0, 0, 0))]
            + [heads_spec] * 3
            + [pieces_spec(place), pieces_spec(first)]
            + [pl.BlockSpec((1, 8, full_len), lambda i, _: (place + i, 0, 0))]
            + [pl.BlockSpec(memory_space=pltpu.VMEM)] * len(sums)
            + [pl.BlockSpec(memory_space=pl.ANY)] * len(after),
            out_specs=(
                pl.BlockSpec((piece_count, 1, block, width), lambda i, _: (0, i, 0, 0)),
                pl.BlockSpec((3 * head_width, width), lambda i, _: (0, 0)),
                pl.BlockSpec((2, 8, head_width), lambda i, _: (0, 0, 0)),
            ),
            scratch_shapes=[
                pltpu.VMEM((head_width, full_len), f32),
                pltpu.VMEM((full_len, head_width), bf16),
                pltpu.VMEM((full_len, head_width), bf16),
            ],
        ),
        compiler_params=pltpu.CompilerParams(vmem_limit_bytes=VMEM_LIMIT),
        cost_estimate=cost(12),
        name="attend_back",
    )(info, *x_parts, weight, query, key, value, mixed, grad, mass, *sums, *after)


def gather_exchange(value, axis):
    count = lax.axis_size(axis)
    spread = jnp.broadcast_to(value[None], (count,) + value.shape)
    return lax.all_to_all(spread, axis, split_axis=0, concat_axis=0, tiled=True)


def gather_relative(value, axis, order):
    pieces = [(0, value)]
    for step in order:
        pieces = pieces + [(offset ^ step, xor_permute(piece, axis, step)) for offset, piece in pieces]
    return pieces


def gather_direct(value, axis):
    count = lax.axis_size(axis)
    return [value] + [xor_permute(value, axis, step) for step in range(1, count)]


def natural(pieces, index):
    return jnp.take(jnp.stack(pieces), index ^ jnp.arange(len(pieces)), axis=0)


def sum_gram(part, after, after_sum):
    low_count = 2
    width = part.shape[0]
    batch_count = lax.axis_size("batch")
    mine = lax.axis_index("seq") % low_count
    two = part.reshape(low_count, width // low_count, width)
    keep = lax.dynamic_index_in_dim(two, mine, 0, keepdims=False)
    send = lax.dynamic_index_in_dim(two, 1 - mine, 0, keepdims=False)
    half, _ = lax.optimization_barrier((keep + xor_permute(send, "seq", 1), after))
    rows = half.shape[0] // batch_count
    chunks = lax.all_to_all(
        half.reshape(batch_count, rows, width), "batch", split_axis=0, concat_axis=0, tiled=True
    )
    own, _ = lax.optimization_barrier((jnp.sum(chunks, axis=0), after_sum))
    return gather_exchange(own, "batch").reshape(half.shape)


def shards(
    inputs,
    counts,
    cotangent,
    attention_weights,
    attention_momenta,
    feed_weights,
    feed_momenta,
    vector_params,
    vector_first,
    vector_second,
):
    seqs, local_len, width = inputs.shape
    seq_count, batch_count = lax.axis_size("seq"), lax.axis_size("batch")
    seq_index, batch_index = lax.axis_index("seq"), lax.axis_index("batch")
    full_len = local_len * seq_count
    tokens_count = seqs * local_len
    head_width = width // seq_count
    head_count = head_width // HEAD_DIM
    column_width = attention_weights.shape[2]
    feed_width = feed_weights.shape[2]
    hidden = feed_width * batch_count * seq_count
    vector_rows = vector_params.shape[0]

    att_own = attention_weights[0].T
    feed_own = feed_weights.transpose(0, 2, 1)
    moment_own = attention_momenta[0].T
    feed_moment_own = feed_momenta.transpose(0, 2, 1)
    vec_low = vector_params.astype(bf16)

    pad = jnp.zeros((16, width), bf16).at[0, : vector_rows * column_width].set(vec_low.reshape(-1))
    feed_payload = jnp.concatenate([feed_own.astype(bf16).reshape(-1, width), pad], axis=0)
    feed_all = lax.all_gather(feed_payload, ("seq", "batch"), axis=0, tiled=False)
    moment_all = lax.all_gather(moment_own, "batch", axis=0, tiled=True)
    x_parts = gather_relative(inputs, "seq", [2, 1])
    x_parts = [piece for _, piece in sorted(x_parts, key=lambda pair: pair[0])]
    payload = jnp.concatenate([att_own.astype(bf16), pad], axis=0)
    member_parts = gather_exchange(payload, "batch")
    member_vecs = member_parts[:, column_width, : vector_rows * column_width]
    member_vecs = member_vecs.reshape(batch_count, vector_rows, column_width)
    member_vecs = member_vecs.transpose(1, 0, 2).reshape(1, vector_rows, width)
    member_vecs = jnp.pad(member_vecs, ((0, 0), (0, 16 - vector_rows), (0, 0)))
    member_rows = member_parts[:, :column_width].reshape(seq_count, head_width, width)
    head_weights = lax.all_to_all(
        jnp.concatenate(
            [member_rows, jnp.broadcast_to(member_vecs, (seq_count, 16, width))], axis=1
        ),
        "seq",
        split_axis=0,
        concat_axis=0,
        tiled=True,
    )
    output_parts = gather_direct(head_weights[3, :head_width], "seq")
    vec_full = feed_all[:, 2 * feed_width, : vector_rows * column_width]
    vec_full = vec_full.reshape(seq_count, batch_count, vector_rows, column_width)
    vec_full = vec_full.transpose(0, 2, 1, 3).reshape(12, width).astype(f32)
    bias_up = vec_full[3:7].reshape(batch_count, seq_count, feed_width)
    bias_up = bias_up.transpose(1, 0, 2).reshape(hidden)

    upper = seq_count // 2
    matrix = seq_index // upper
    moment_send = lax.dynamic_index_in_dim(feed_moment_own, 1 - matrix, 0, keepdims=False)
    moment_keep = lax.dynamic_index_in_dim(feed_moment_own, matrix, 0, keepdims=False)
    moment_other = xor_permute(moment_send, "seq", upper)

    info = jnp.concatenate([seq_index.astype(jnp.int32)[None], counts])
    ranges = ((0, 1), (1, seqs - 1))
    saved, mixed_tok = [], []
    for turn, (first, count) in enumerate(ranges):
        saved.append(
            attend(info, x_parts, head_weights, first, count, output_parts[1:] if turn else ())
        )
        mixed_tok.append(
            lax.all_to_all(saved[-1][3], "seq", split_axis=0, concat_axis=0, tiled=True)
        )

    (
        grad_mixed,
        layer_out,
        gate,
        grad_up,
        normed,
        grad_down,
        grad_attn,
        mixed_flat,
        grad_rest,
        vec_sums,
        up_sums,
    ) = token_part(
        info, inputs, mixed_tok, cotangent, feed_all, vec_full, bias_up[None], output_parts, ranges
    )
    grad_heads = lax.all_to_all(grad_mixed, "seq", split_axis=0, concat_axis=0, tiled=True)
    pair_keep, pair_send = feed_grads(info, gate, grad_up, normed, grad_down, seq_count)

    pair_send, grad_heads = lax.optimization_barrier((pair_send, grad_heads))
    pair_sum = (pair_keep.astype(f32) + xor_permute(pair_send, "seq", 1).astype(f32)).astype(bf16)
    cross_keep = lax.dynamic_index_in_dim(pair_sum, matrix, 0, keepdims=False)
    cross_send = lax.dynamic_index_in_dim(pair_sum, 1 - matrix, 0, keepdims=False)
    cross_got = xor_permute(cross_send, "seq", upper)
    sums, backs = (), []
    for first in range(seqs):
        part = 0 if first < ranges[0][1] else 1
        if first == seqs - 1:
            cross_got, _ = lax.optimization_barrier((cross_got, backs[-1]))
            cross_sum = cross_keep.astype(f32) + cross_got.astype(f32)
            cross_sum = cross_sum.astype(bf16).reshape(2, batch_count, feed_width, width)
        back, *sums = attend_back(
            info,
            x_parts,
            head_weights,
            saved[part],
            grad_heads,
            first,
            first - ranges[part][0],
            sums,
            (pair_sum,) if first == 0 else (cross_sum, moment_all) if first == seqs - 1 else (),
        )
        backs.append(back)
    head_weight_grads, head_bias_grads = sums
    back_part = jnp.concatenate(backs, axis=1)
    low_half = [back_part[0].astype(f32), back_part[upper].astype(f32)]
    low_got = xor_permute(jnp.stack([back_part[1], back_part[upper + 1]]), "seq", 1).astype(f32)
    high_got = xor_permute((low_half[1] + low_got[1]).astype(bf16), "seq", upper).astype(f32)
    grad_tokens = grad_rest.reshape(inputs.shape)
    input_grad = (grad_tokens + low_half[0] + low_got[0] + high_got).astype(bf16)

    feed_chunks = lax.all_to_all(
        cross_sum.transpose(1, 0, 2, 3), "batch", split_axis=0, concat_axis=0, tiled=True
    )
    feed_sum = jnp.sum(feed_chunks.astype(f32), axis=0)
    mine_first = matrix == 0
    moment_pair = jnp.where(
        mine_first, jnp.stack([moment_keep, moment_other]), jnp.stack([moment_other, moment_keep])
    )
    feed_moment_pair = muon_decay * moment_pair + feed_sum
    feed_rows = feed_moment_pair.reshape(2 * feed_width, width)
    gram_part = gram(feed_rows)

    mixed_flat, _ = lax.optimization_barrier((mixed_flat, backs[0]))
    grad_w_output = dot(grad_attn, mixed_flat, TN).astype(bf16)
    output_rows = grad_w_output.reshape(seq_count, head_width, width)
    output_sum = lax.dynamic_index_in_dim(output_rows, seq_index, 0, keepdims=False).astype(f32)
    for step in range(1, seq_count):
        part = lax.dynamic_index_in_dim(output_rows, seq_index ^ step, 0, keepdims=False)
        output_sum = output_sum + xor_permute(part, "seq", step).astype(f32)
    att_grads = jnp.concatenate([head_weight_grads.astype(bf16), output_sum.astype(bf16)])
    att_grads = att_grads.reshape(seq_count, batch_count, -1, width).transpose(1, 0, 2, 3)

    def at_heads(grad):
        return lax.dynamic_update_slice(
            jnp.zeros((width,), f32), grad[0], (seq_index * head_width,)
        )

    grad_bias_up = up_sums[0].reshape(seq_count, batch_count, feed_width)
    vec_grads = jnp.concatenate(
        [
            jnp.stack([at_heads(head_bias_grads[0]), at_heads(head_bias_grads[1]), vec_sums[0]]),
            grad_bias_up.transpose(1, 0, 2).reshape(4, width),
            vec_sums[1:6],
        ]
    )
    vec_grads = vec_grads.astype(bf16).reshape(seq_count, vector_rows, batch_count, column_width)
    vec_grads = vec_grads.transpose(2, 0, 1, 3).reshape(batch_count, seq_count, -1)
    att_rows = att_grads.shape[2]
    vec_grads = jnp.pad(vec_grads, ((0, 0), (0, 0), (0, att_rows * 128 - vec_grads.shape[2])))
    vec_grads = vec_grads.reshape(batch_count, seq_count, att_rows, 128)
    everywhere = ("batch", "seq")
    att_got = lax.all_to_all(
        jnp.concatenate([att_grads, vec_grads], axis=3).reshape(
            batch_count * seq_count, att_rows, width + 128
        ),
        everywhere,
        split_axis=0,
        concat_axis=0,
        tiled=True,
    )
    att_got = att_got.reshape(batch_count, seq_count, att_rows, width + 128)
    att_sum = jnp.sum(att_got[..., :width].astype(f32), axis=0).astype(bf16)
    att_pieces = gather_direct(att_sum, "batch")
    att_rows_own, ortho_att = newton_whole(
        batch_index, att_pieces, moment_all, column_width, input_grad
    )
    grad_vec = jnp.sum(att_got[..., width:].astype(f32), axis=(0, 1)).reshape(-1)
    grad_vec = grad_vec[: vector_rows * column_width].reshape(vector_rows, column_width)
    gram_half = sum_gram(gram_part, att_got, att_pieces)
    gram_half, _ = lax.optimization_barrier((gram_half, ortho_att))
    gram_other = xor_permute(gram_half, "seq", 1)
    ortho_feed_pair = newton(info, gram_half, gram_other, feed_rows)
    ortho_feed_pair = ortho_feed_pair.reshape(2, feed_width, width)
    ortho_att, att_rows_own, ortho_feed_pair = lax.optimization_barrier(
        (ortho_att, att_rows_own, ortho_feed_pair)
    )
    both_pair = jnp.stack([feed_moment_pair, ortho_feed_pair], axis=1)
    both_keep = lax.dynamic_index_in_dim(both_pair, matrix, 0, keepdims=False)
    both_send = lax.dynamic_index_in_dim(both_pair, 1 - matrix, 0, keepdims=False)
    both_other = xor_permute(both_send, "seq", upper)
    both = jnp.where(
        mine_first, jnp.stack([both_keep, both_other], 1), jnp.stack([both_other, both_keep], 1)
    )
    feed_moment = both[0].transpose(0, 2, 1)
    ortho_feed = both[1].transpose(0, 2, 1)

    attention_moment = att_rows_own.T[None]
    ortho_att = ortho_att.T[None]
    attention_next = attention_weights * (1.0 - muon_rate * decay_rate) - muon_rate * ortho_att
    feed_next = feed_weights * (1.0 - muon_rate * decay_rate) - muon_rate * ortho_feed
    vector_first_next = beta_one * vector_first + (1.0 - beta_one) * grad_vec
    vector_second_next = beta_two * vector_second + (1.0 - beta_two) * grad_vec * grad_vec
    first_hat = vector_first_next / (1.0 - beta_one**STEP)
    second_hat = vector_second_next / (1.0 - beta_two**STEP)
    vector_next = vector_params * (1.0 - adam_rate * decay_rate) - adam_rate * first_hat / (
        jnp.sqrt(second_hat) + adam_eps
    )
    return (
        layer_out,
        input_grad,
        attention_next,
        attention_moment,
        feed_next,
        feed_moment,
        vector_next,
        vector_first_next,
        vector_second_next,
    )


def solution(mesh):
    tokens_spec = P("batch", "seq", None)
    attention_spec = P("seq", None, "batch")
    feed_spec = P(None, None, ("batch", "seq"))
    vector_spec = P("seq", "batch")
    return jax.shard_map(
        shards,
        mesh=mesh,
        in_specs=(tokens_spec, P("batch"), tokens_spec)
        + (attention_spec,) * 2
        + (feed_spec,) * 2
        + (vector_spec,) * 3,
        out_specs=(tokens_spec,) * 2
        + (attention_spec,) * 2
        + (feed_spec,) * 2
        + (vector_spec,) * 3,
        check_vma=False,
    )
```

```python
import functools

import jax
import jax.numpy as jnp
from jax import lax
from jax.experimental import pallas as pl
from jax.experimental.pallas import tpu as pltpu
from jax.sharding import PartitionSpec as P

HEAD_DIM = 64
STEP = 10
NS_STEPS = 5

newton_coef = (3.4445, -4.775, 2.0315)
muon_rate = 0.6
muon_decay = 0.95
adam_rate = 0.3
beta_one = 0.9
beta_two = 0.999
decay_rate = 0.01
adam_eps = 1e-08
norm_eps = 1e-05
masked_score = -1e30
bf16 = jnp.bfloat16
f32 = jnp.float32
MIB = 1024 * 1024


def cost(micros):
    return pl.CostEstimate(flops=int(micros * 1.15e9), bytes_accessed=1 << 20, transcendentals=0)

NN = (((1,), (0,)), ((), ()))
NT = (((1,), (1,)), ((), ()))
TN = (((0,), (0,)), ((), ()))


def dot(left, right, dims=NN):
    return lax.dot_general(left, right, dims, preferred_element_type=f32)


def xor_permute(value, axis, step):
    count = lax.axis_size(axis)
    return lax.ppermute(value, axis, [(i, i ^ step) for i in range(count)])


def halves(value):
    high = value.astype(bf16)
    return high, (value - high.astype(f32)).astype(bf16)


def dot_split(left, right, dims=NN):
    (left_high, left_low), (right_high, right_low) = left, right
    return (
        dot(left_high, right_high, dims)
        + dot(left_high, right_low, dims)
        + dot(left_low, right_high, dims)
    )


def dot_split_wide(left, right):
    (left_high, left_low), (right_high, right_low) = left, right
    return dot(
        jnp.concatenate([left_high, left_high, left_low], axis=1),
        jnp.concatenate([right_high, right_low, right_high], axis=0),
    )


def newton_loop(square, rows):
    width = square.shape[0]
    for turn in range(NS_STEPS):
        square_parts, row_parts = halves(square), halves(rows)
        squared = dot_split_wide(square_parts, square_parts)
        poly_parts = halves(newton_coef[1] * square + newton_coef[2] * squared)
        if turn + 1 == NS_STEPS:
            return newton_coef[0] * rows + dot_split_wide(row_parts, poly_parts)
        both = [jnp.concatenate(pair, axis=0) for pair in zip(square_parts, row_parts)]
        made = dot_split_wide(both, poly_parts)
        rows = newton_coef[0] * rows + made[width:]
        once = newton_coef[0] * square + made[:width]
        square = newton_coef[0] * once + dot_split_wide(halves(once), poly_parts)


def gram_of_rows(rows):
    parts = halves(rows)
    return dot_split(parts, parts, TN)


def normalized(gram, rows):
    width = gram.shape[0]
    shape = (width, width)
    on_diagonal = lax.broadcasted_iota(jnp.int32, shape, 0) == lax.broadcasted_iota(
        jnp.int32, shape, 1
    )
    trace = jnp.sum(jnp.where(on_diagonal, gram, 0.0), keepdims=True)
    factor = 1.0 / (jnp.sqrt(trace) + 1e-07)
    return gram * (factor * factor), rows * factor


def gram_kernel(info_ref, rows_ref, *refs):
    total_ref = refs[2]
    total_ref[...] = gram_of_rows(rows_ref[...])
    for distance, out_ref in enumerate(refs[:2]):
        size = out_ref.shape[0]
        start = pl.multiple_of(((info_ref[0] % 2) ^ distance) * size, size)
        out_ref[...] = total_ref[pl.ds(start, size), :]


def gram(info, rows):
    width = rows.shape[1]
    half = jax.ShapeDtypeStruct((width // 2, width), f32)
    vmem = pl.BlockSpec(memory_space=pltpu.VMEM)
    return pl.pallas_call(
        gram_kernel,
        out_shape=(half, half),
        in_specs=[pl.BlockSpec(memory_space=pltpu.SMEM), vmem],
        out_specs=(vmem, vmem),
        scratch_shapes=[pltpu.VMEM((width, width), f32)],
        compiler_params=pltpu.CompilerParams(vmem_limit_bytes=10 * MIB),
        cost_estimate=cost(2),
        name="gram",
    )(info, rows)


def deal_kernel(index_ref, left_ref, right_ref, *out_refs):
    size = out_refs[0].shape[1]
    for side, out_ref in enumerate(out_refs):
        for distance in range(out_ref.shape[0]):
            block = index_ref[0] ^ (2 * distance + side)
            rows = pl.ds(pl.multiple_of(block * size, size), size)
            out_ref[distance] = left_ref[rows, :] + right_ref[rows, :]


def deal(index, left, right, count):
    rows = left.shape[0] // count
    if rows % 8:
        total = jnp.take((left + right).reshape(count, rows, -1), index ^ jnp.arange(count), axis=0)
        return total[0::2], total[1::2]
    vmem = pl.BlockSpec(memory_space=pltpu.VMEM)
    shape = jax.ShapeDtypeStruct((count // 2, rows, left.shape[1]), left.dtype)
    return pl.pallas_call(
        deal_kernel,
        out_shape=(shape, shape),
        in_specs=[pl.BlockSpec(memory_space=pltpu.SMEM), vmem, vmem],
        out_specs=(vmem, vmem),
        compiler_params=pltpu.CompilerParams(vmem_limit_bytes=6 * MIB),
        cost_estimate=cost(1),
        name="deal",
    )(index[None].astype(jnp.int32), left, right)


def newton_kernel(place_ref, *refs):
    rows_ref, _, out_ref, square_ref = refs[-4:]
    half = square_ref.shape[0] // 2
    parts = refs[:-4]
    for turn, part_ref in enumerate(parts):
        distance, side = turn % (len(parts) // 2), turn // (len(parts) // 2)
        size = part_ref.shape[0]
        place = (place_ref[0] ^ distance) * size if len(parts) > 2 else 0
        start = pl.multiple_of(((place_ref[1] % 2) ^ side) * half + place, 8)
        square_ref[pl.ds(start, size), :] = part_ref[...]
    out_ref[...] = newton_loop(*normalized(square_ref[...], rows_ref[...]))


def newton(batch_index, seq_index, mine, other, rows, after):
    width = rows.shape[1]
    if mine[0].shape[0] % 8:
        mine = [natural(mine, batch_index).reshape(-1, width)]
        other = [natural(other, batch_index).reshape(-1, width)]
    place = jnp.stack([batch_index, seq_index]).astype(jnp.int32)
    vmem = pl.BlockSpec(memory_space=pltpu.VMEM)
    return pl.pallas_call(
        newton_kernel,
        out_shape=jax.ShapeDtypeStruct(rows.shape, f32),
        in_specs=[pl.BlockSpec(memory_space=pltpu.SMEM)]
        + [vmem] * (len(mine) + len(other) + 1)
        + [pl.BlockSpec(memory_space=pl.ANY)],
        out_specs=vmem,
        scratch_shapes=[pltpu.VMEM((width, width), f32)],
        compiler_params=pltpu.CompilerParams(vmem_limit_bytes=20 * MIB),
        cost_estimate=cost(15),
        name="newton",
    )(place, *mine, *other, rows, after)


def newton_whole_kernel(index_ref, *refs, count):
    pieces, (old_ref, _, moment_ref, out_ref, rows_ref) = refs[:count], refs[count:]
    own = moment_ref.shape[0]
    members, step = pieces[0].shape[:2]
    stride = rows_ref.shape[0] // members
    for turn in range(count):
        place = (index_ref[0] ^ turn) * step if count > 1 else 0
        for member in range(members):
            rows = pl.ds(member * stride + pl.multiple_of(place, 8), step)
            rows_ref[rows, :] = muon_decay * old_ref[rows, :] + pieces[turn][member].astype(f32)
    gram = gram_of_rows(rows_ref[...])
    rows = rows_ref[pl.ds(pl.multiple_of(index_ref[0] * own, 8), own), :]
    moment_ref[...] = rows
    out_ref[...] = newton_loop(*normalized(gram, rows))


def newton_whole(index, pieces, old, own, after):
    if pieces[0].shape[1] % 8:
        pieces = [natural(pieces, index).transpose(1, 0, 2, 3).reshape(1, *old.shape)]
    shape = jax.ShapeDtypeStruct((own, old.shape[1]), f32)
    return pl.pallas_call(
        functools.partial(newton_whole_kernel, count=len(pieces)),
        out_shape=(shape, shape),
        in_specs=[pl.BlockSpec(memory_space=pltpu.SMEM)]
        + [pl.BlockSpec(memory_space=pltpu.VMEM)] * (len(pieces) + 1)
        + [pl.BlockSpec(memory_space=pl.ANY)],
        out_specs=(pl.BlockSpec(memory_space=pltpu.VMEM),) * 2,
        scratch_shapes=[pltpu.VMEM(old.shape, f32)],
        compiler_params=pltpu.CompilerParams(vmem_limit_bytes=22 * MIB),
        cost_estimate=cost(17),
        name="newton_whole",
    )(index[None].astype(jnp.int32), *pieces, old, after)


def norm_parts(values_in):
    centre = values_in - jnp.mean(values_in, axis=-1, keepdims=True)
    inverse_dev = lax.rsqrt(jnp.mean(centre * centre, axis=-1, keepdims=True) + norm_eps)
    return centre * inverse_dev, inverse_dev


def norm_back(grad, normal, inverse_dev, gain):
    scaled = grad * gain
    mean_scaled = jnp.mean(scaled, axis=-1, keepdims=True)
    mean_normal = jnp.mean(scaled * normal, axis=-1, keepdims=True)
    return inverse_dev * (scaled - mean_scaled - normal * mean_normal)


def column_sum(values_in):
    return jnp.sum(values_in.astype(f32), axis=0, keepdims=True)


def token_kernel(info_ref, x_ref, cotangent_ref, feed_ref, vec_ref, up_bias_ref, *refs, ranges):
    seqs, block, width = x_ref.shape
    mixed_refs, refs = refs[: len(ranges)], refs[len(ranges) :]
    seq_count = mixed_refs[0].shape[0]
    output_refs, refs = refs[:seq_count], refs[seq_count:]
    grad_mixed_ref, refs = refs[0], refs[1:]
    out_ref, gate_ref, up_grad_ref, normed_ref, down_grad_ref = refs[:5]
    attn_grad_ref, mixed_flat_ref, rest_ref, sums_ref, up_sums_ref = refs[5:10]
    w_output_ref, slope_ref = refs[10:]
    tokens = seqs * block
    head_width = width // seq_count
    pieces, feed_width = feed_ref.shape[0], (feed_ref.shape[1] - 16) // 2
    chunk_pieces = max(1, pieces // 4)
    chunk = chunk_pieces * feed_width
    chunks = pieces // chunk_pieces

    def weights(matrix, i):
        rows = slice(matrix * feed_width, (matrix + 1) * feed_width)
        return feed_ref[i * chunk_pieces : (i + 1) * chunk_pieces, rows].reshape(chunk, width)

    def vec(row):
        return vec_ref[row : row + 1]

    for offset in range(seq_count):
        start = pl.multiple_of((info_ref[0] ^ offset) * head_width, head_width)
        w_output_ref[pl.ds(start, head_width), :] = output_refs[offset][...]
    for place in range(seq_count):
        lanes = slice(place * head_width, (place + 1) * head_width)
        for mixed_ref, (first, count) in zip(mixed_refs, ranges):
            rows = slice(first * block, (first + count) * block)
            mixed_flat_ref[rows, lanes] = mixed_ref[place].reshape(count * block, head_width)
    x = x_ref[...].reshape(tokens, width).astype(f32)
    attn_out = dot(mixed_flat_ref[...], w_output_ref[...], NT) + vec(2)
    normal_first, inverse_first = norm_parts(x + attn_out)
    normed = normal_first * vec(8) + vec(9)
    normed_low = normed.astype(bf16)
    normed_ref[...] = normed_low
    down_out = vec(7)
    curve, cubic = (2.0 / jnp.pi) ** 0.5, 0.044715
    for i in range(chunks):
        lanes = slice(i * chunk, (i + 1) * chunk)
        up = dot(normed_low, weights(0, i), NT) + up_bias_ref[:, lanes]
        square = up * up
        bend = jnp.tanh(up * (curve + (curve * cubic) * square))
        half = 0.5 + 0.5 * bend
        gate = (up * half).astype(bf16)
        gate_ref[:, lanes] = gate
        slope_ref[:, lanes] = half + (0.5 * up) * (1.0 - bend * bend) * (
            curve + (3.0 * curve * cubic) * square
        )
        down_out = down_out + dot(gate, weights(1, i))
    normal_second, inverse_second = norm_parts(x + normed + down_out)
    out = normal_second * vec(10) + vec(11)
    out_ref[...] = out.astype(bf16).reshape(out_ref.shape)
    grad_out = cotangent_ref[...].reshape(tokens, width).astype(f32)
    grad_sum = norm_back(grad_out, normal_second, inverse_second, vec(10))
    sums_ref[4:5] = column_sum(grad_out * normal_second)
    sums_ref[5:6] = column_sum(grad_out)
    grad_down_low = grad_sum.astype(bf16)
    down_grad_ref[...] = grad_down_low
    sums_ref[1:2] = column_sum(grad_down_low)
    grad_normed = grad_sum
    for i in range(chunks):
        lanes = slice(i * chunk, (i + 1) * chunk)
        grad_up = dot(grad_down_low, weights(1, i), NT) * slope_ref[:, lanes]
        grad_up_low = grad_up.astype(bf16)
        up_grad_ref[:, lanes] = grad_up_low
        up_sums_ref[0:1, lanes] = column_sum(grad_up_low)
        grad_normed = grad_normed + dot(grad_up_low, weights(0, i))
    grad_first = norm_back(grad_normed, normal_first, inverse_first, vec(8))
    sums_ref[2:3] = column_sum(grad_normed * normal_first)
    sums_ref[3:4] = column_sum(grad_normed)
    grad_attn_low = grad_first.astype(bf16)
    attn_grad_ref[...] = grad_attn_low
    sums_ref[0:1] = column_sum(grad_attn_low)
    rest_ref[...] = grad_sum + grad_first
    grad_mixed = dot(grad_attn_low, w_output_ref[...]).astype(bf16)
    for place in range(seq_count):
        lanes = slice(place * head_width, (place + 1) * head_width)
        grad_mixed_ref[place] = grad_mixed[:, lanes].reshape(seqs, block, head_width)


def token_part(info, x, mixed, cotangent, feed_all, vec_full, up_bias, output_parts, ranges):
    seqs, block, width = x.shape
    tokens = seqs * block
    if (feed_all.shape[1] - 16) // 2 % 16:
        rows = (feed_all.shape[1] - 16) // 2
        parts = [feed_all[:, i * rows : (i + 1) * rows].reshape(-1, width) for i in range(2)]
        feed_all = jnp.concatenate(parts + [jnp.zeros((16, width), bf16)])[None]
    hidden = up_bias.shape[1]

    def shape(*dims, kind=bf16):
        return jax.ShapeDtypeStruct(dims, kind)

    vmem = pl.BlockSpec(memory_space=pltpu.VMEM)
    return pl.pallas_call(
        functools.partial(token_kernel, ranges=ranges),
        out_shape=(
            shape(mixed[0].shape[0], seqs, block, mixed[0].shape[3]),
            shape(seqs, block, width),
            shape(tokens, hidden),
            shape(tokens, hidden),
            shape(tokens, width),
            shape(tokens, width),
            shape(tokens, width),
            shape(tokens, width),
            shape(tokens, width, kind=f32),
            shape(8, width, kind=f32),
            shape(8, hidden, kind=f32),
        ),
        in_specs=[pl.BlockSpec(memory_space=pltpu.SMEM)] + [vmem] * (5 + len(mixed) + len(output_parts)),
        out_specs=(vmem,) * 11,
        scratch_shapes=[pltpu.VMEM((width, width), bf16), pltpu.VMEM((tokens, hidden), f32)],
        compiler_params=pltpu.CompilerParams(vmem_limit_bytes=60 * MIB),
        cost_estimate=cost(17),
        name="token_part",
    )(info, x, cotangent, feed_all, vec_full, up_bias, *mixed, *output_parts)


def weight_grad_kernel(info_ref, *refs):
    gate_ref, grad_up_ref, normed_ref, grad_down_ref, grad_attn_ref, mixed_ref = refs[:6]
    pair_refs, output_refs = refs[6:8], refs[8:]
    upper, rows = pair_refs[0].shape[1:3]
    for distance, out_ref in enumerate(output_refs):
        size = out_ref.shape[0]
        lanes = pl.ds(pl.multiple_of((info_ref[0] ^ distance) * size, size), size)
        out_ref[...] = dot(grad_attn_ref[:, lanes], mixed_ref[...], TN).astype(bf16)
    for distance, out_ref in enumerate(pair_refs):
        for part in range(upper):
            block = part * 2 + ((info_ref[0] % 2) ^ distance)
            lanes = pl.ds(pl.multiple_of(block * rows, rows), rows)
            made = dot(grad_up_ref[:, lanes], normed_ref[...], TN)
            out_ref[0, part] = made.astype(bf16)
            made = dot(gate_ref[:, lanes], grad_down_ref[...], TN)
            out_ref[1, part] = made.astype(bf16)


def weight_grads(info, gate, grad_up, normed, grad_down, grad_attn, mixed, seq_count):
    hidden, width = gate.shape[1], normed.shape[1]
    pair = jax.ShapeDtypeStruct((2, seq_count // 2, hidden // seq_count, width), bf16)
    output = jax.ShapeDtypeStruct((width // seq_count, width), bf16)
    vmem = pl.BlockSpec(memory_space=pltpu.VMEM)
    keep, send, *outputs = pl.pallas_call(
        weight_grad_kernel,
        out_shape=(pair,) * 2 + (output,) * seq_count,
        in_specs=[pl.BlockSpec(memory_space=pltpu.SMEM)] + [vmem] * 6,
        out_specs=(vmem,) * (2 + seq_count),
        compiler_params=pltpu.CompilerParams(vmem_limit_bytes=60 * MIB),
        cost_estimate=cost(1),
        name="weight_grads",
    )(info, gate, grad_up, normed, grad_down, grad_attn, mixed)
    return keep, send, outputs


def attend_kernel(info_ref, *refs, piece_count, head_width, first):
    x_refs, weight_ref = refs[:piece_count], refs[piece_count]
    query_ref, key_ref, value_ref, mixed_ref, mass_ref, query_t_ref, value_t_ref = refs[-7:]
    seq_index, length = info_ref[0], info_ref[1 + first + pl.program_id(0)]
    block = x_refs[0].shape[1]
    heads = head_width // HEAD_DIM
    value_rows = value_t_ref.shape[0] // heads
    own_lanes = pl.ds(pl.multiple_of(seq_index * head_width, head_width), head_width)
    vecs = weight_ref[0, head_width:, own_lanes].astype(f32)
    ones = jnp.ones((value_rows - HEAD_DIM, block), bf16)
    for offset in range(piece_count):
        rows = pl.ds(pl.multiple_of((seq_index ^ offset) * block, block), block)
        x = x_refs[offset][0]
        query = dot(x, weight_ref[0, :head_width], NT) + vecs[0:1]
        query = query.astype(bf16) * jnp.asarray(HEAD_DIM**-0.5, bf16)
        query_ref[0, rows, :] = query
        query_t_ref[:, rows] = query.T
        key_ref[0, rows, :] = dot(x, weight_ref[1, :head_width], NT).astype(bf16)
        value = (dot(x, weight_ref[2, :head_width], NT) + vecs[1:2]).astype(bf16)
        value_ref[0, rows, :] = value
        value_t = value.T
        for head in range(heads):
            start = head * value_rows
            value_t_ref[start : start + HEAD_DIM, rows] = value_t[
                head * HEAD_DIM : (head + 1) * HEAD_DIM
            ]
            value_t_ref[start + HEAD_DIM : start + value_rows, rows] = ones
    live_blocks = (length + block - 1) // block

    full_len = piece_count * block
    span = full_len

    def attend_blocks(count):
        for start in range(0, full_len, span):
            rows = slice(start, start + span)
            outs = []
            for head in range(heads):
                lanes = slice(head * HEAD_DIM, (head + 1) * HEAD_DIM)
                query_t = query_t_ref[lanes, rows]
                tiles = []
                top = None
                for i in range(count):
                    tile = dot(key_ref[0, i * block : (i + 1) * block, lanes], query_t)
                    if i == count - 1:
                        live = lax.broadcasted_iota(jnp.int32, tile.shape, 0) + i * block < length
                        tile = jnp.where(live, tile, masked_score)
                    tiles.append(tile)
                    tile_top = jnp.max(tile, axis=0, keepdims=True)
                    top = tile_top if top is None else jnp.maximum(top, tile_top)
                value_span = slice(head * value_rows, (head + 1) * value_rows)
                tiles = [jnp.exp(tile - top).astype(bf16) for tile in tiles]
                mixed = dot(
                    value_t_ref[value_span, : count * block], jnp.concatenate(tiles, axis=0)
                )
                mass = mixed[HEAD_DIM : HEAD_DIM + 1]
                outs.append(mixed[:HEAD_DIM] / mass)
                mass_ref[0, head : head + 1, rows] = top + jnp.log(mass)
            outs = jnp.concatenate(outs, axis=0).astype(bf16).T
            mixed_ref[start // block : (start + span) // block, 0] = outs.reshape(
                span // block, block, head_width
            )

    for count in range(1, piece_count + 1):
        pl.when(live_blocks == count)(functools.partial(attend_blocks, count))


def attend(info, x_parts, weight, first, seqs, after):
    piece_count = len(x_parts)
    _, block, width = x_parts[0].shape
    head_width = width // piece_count
    full_len = piece_count * block
    heads_shape = jax.ShapeDtypeStruct((seqs, full_len, head_width), bf16)
    heads_spec = pl.BlockSpec((1, full_len, head_width), lambda i, _: (i, 0, 0))
    return pl.pallas_call(
        functools.partial(
            attend_kernel, piece_count=piece_count, head_width=head_width, first=first
        ),
        out_shape=(heads_shape,) * 3
        + (
            jax.ShapeDtypeStruct((piece_count, seqs, block, head_width), bf16),
            jax.ShapeDtypeStruct((seqs, 8, full_len), f32),
        ),
        grid_spec=pltpu.PrefetchScalarGridSpec(
            num_scalar_prefetch=1,
            grid=(seqs,),
            in_specs=[pl.BlockSpec((1, block, width), lambda i, _: (first + i, 0, 0))] * piece_count
            + [pl.BlockSpec(weight.shape, lambda i, _: (0, 0, 0))]
            + [pl.BlockSpec(memory_space=pl.ANY)] * len(after),
            out_specs=(heads_spec,) * 3
            + (
                pl.BlockSpec((piece_count, 1, block, head_width), lambda i, _: (0, i, 0, 0)),
                pl.BlockSpec((1, 8, full_len), lambda i, _: (i, 0, 0)),
            ),
            scratch_shapes=[
                pltpu.VMEM((head_width, full_len), bf16),
                pltpu.VMEM((head_width // HEAD_DIM * (HEAD_DIM + 16), full_len), bf16),
            ],
        ),
        compiler_params=pltpu.CompilerParams(vmem_limit_bytes=60 * MIB),
        cost_estimate=cost(7 * seqs),
        name="attend",
    )(info, *x_parts, weight, *after)


def attend_back_kernel(info_ref, *refs, piece_count, head_width, first, sum_count, after_count):
    x_refs, refs = refs[:piece_count], refs[piece_count:]
    weight_ref, query_ref, key_ref, value_ref, mixed_ref, grad_ref, mass_ref = refs[:7]
    sum_refs, refs = refs[7 : 7 + sum_count], refs[7 + sum_count + after_count :]
    back_refs, weight_out_ref, bias_grad_ref, query_acc, key_acc, value_acc = refs[:2], *refs[2:7]
    query_t_ref, grad_t_ref, key_t_ref = refs[7:10]
    weight_grad_ref = refs[10] if refs[10:] else weight_out_ref
    step = pl.program_id(0)
    seq_index, length = info_ref[0], info_ref[1 + first + step]
    block = x_refs[0].shape[1]
    scale = HEAD_DIM**-0.5
    live_blocks = (length + block - 1) // block
    heads = head_width // HEAD_DIM
    query_acc[...] = jnp.zeros_like(query_acc)

    inner = []
    head_of_lane = lax.broadcasted_iota(jnp.int32, (8, head_width), 1) // HEAD_DIM
    picks = (head_of_lane == lax.broadcasted_iota(jnp.int32, (8, head_width), 0)).astype(bf16)
    for place in range(piece_count):
        columns = slice(place * block, (place + 1) * block)
        grad = grad_ref[place, 0]
        product = mixed_ref[place, 0].astype(f32) * grad.astype(f32)
        high, low = halves(product)
        inner.append(dot(picks, high, NT) + dot(picks, low, NT))
        query_t_ref[:, columns] = query_ref[0, columns, :].T
        key_t_ref[:, columns] = key_ref[0, columns, :].T
        grad_t_ref[:, columns] = grad.T

    inner = jnp.concatenate(inner, axis=1)
    full_len = piece_count * block
    span = full_len

    def key_block(k, masked):
        rows = pl.ds(pl.multiple_of(k * block, block), block)
        key_out, value_out = [], []
        for head in range(heads):
            lanes = slice(head * HEAD_DIM, (head + 1) * HEAD_DIM)
            key, value, key_t = key_ref[0, rows, lanes], value_ref[0, rows, lanes], key_t_ref[lanes, rows]
            key_grad, value_grad = None, None
            for start in range(0, full_len, span):
                columns = slice(start, start + span)
                tile = dot(key, query_t_ref[lanes, columns]) - mass_ref[0, head : head + 1, columns]
                if masked:
                    live = lax.broadcasted_iota(jnp.int32, tile.shape, 0) + k * block < length
                    tile = jnp.where(live, tile, masked_score)
                weights = jnp.exp(tile)
                tile = dot(value, grad_t_ref[lanes, columns]) - inner[head : head + 1, columns]
                score_grad = (weights * tile).astype(bf16)
                grad = grad_ref[start // block : (start + span) // block, 0, :, lanes]
                part = dot(weights.astype(bf16), grad.reshape(span, HEAD_DIM))
                value_grad = part if value_grad is None else value_grad + part
                part = dot(score_grad, query_ref[0, columns, lanes])
                key_grad = part if key_grad is None else key_grad + part
                query_acc[lanes, columns] += dot(key_t, score_grad)
            key_out.append(key_grad)
            value_out.append(value_grad)
        key_acc[rows, :] = jnp.concatenate(key_out, axis=1).astype(bf16)
        value_acc[rows, :] = jnp.concatenate(value_out, axis=1).astype(bf16)

    @pl.loop(0, live_blocks - 1)
    def _(k):
        key_block(k, False)

    key_block(live_blocks - 1, True)

    @pl.loop(live_blocks, piece_count)
    def _(k):
        rows = pl.ds(pl.multiple_of(k * block, block), block)
        key_acc[rows, :] = jnp.zeros((block, head_width), bf16)
        value_acc[rows, :] = jnp.zeros((block, head_width), bf16)

    @pl.when(step == 0)
    def _():
        if sum_refs:
            weight_grad_ref[...] = sum_refs[0][...]
            bias_grad_ref[...] = sum_refs[1][...]
        else:
            weight_grad_ref[...] = jnp.zeros_like(weight_grad_ref)
            bias_grad_ref[...] = jnp.zeros_like(bias_grad_ref)

    ones = jnp.ones((8, block), bf16)
    for offset in range(piece_count):
        start = pl.multiple_of((seq_index ^ offset) * block, block)
        rows = pl.ds(start, block)
        query_grad_t = (query_acc[:, rows] * scale).astype(bf16)
        query_grad = query_grad_t.T
        key_grad, value_grad = key_acc[rows, :], value_acc[rows, :]
        x = x_refs[offset][0]
        weight_grad_ref[:head_width] += dot(query_grad_t, x)
        weight_grad_ref[head_width : 2 * head_width] += dot(key_grad, x, TN)
        weight_grad_ref[2 * head_width :] += dot(value_grad, x, TN)
        bias_grad_ref[0] += dot(ones, query_grad)
        bias_grad_ref[1] += dot(ones, value_grad)
        back = dot(query_grad, weight_ref[0, :head_width])
        back = back + dot(key_grad, weight_ref[1, :head_width])
        back = back + dot(value_grad, weight_ref[2, :head_width])
        back_refs[offset % 2][offset // 2, 0] = back.astype(bf16)
    if weight_grad_ref is not weight_out_ref:
        weight_out_ref[...] = weight_grad_ref[...].astype(bf16)


def attend_back(info, x_parts, weight, saved, grad, first, place, before, after, last):
    piece_count = len(x_parts)
    _, block, width = x_parts[0].shape
    head_width = width // piece_count
    full_len = piece_count * block
    query, key, value, mixed, mass = saved
    seqs, all_seqs = 1, x_parts[0].shape[0]
    backs, sums = before[:2], before[2:]
    back_shape = jax.ShapeDtypeStruct((piece_count // 2, all_seqs, block, width), bf16)
    back_spec = pl.BlockSpec((piece_count // 2, 1, block, width), lambda i, _: (0, first + i, 0, 0))
    weight_shape = (3 * head_width, width)
    after = (*after, *backs)
    inputs_count = 1 + piece_count + 1 + 3 + 2 + 1 + len(sums) + len(after)
    heads_spec = pl.BlockSpec((1, full_len, head_width), lambda i, _: (place + i, 0, 0))

    def pieces_spec(row):
        return pl.BlockSpec((piece_count, 1, block, head_width), lambda i, _: (0, row + i, 0, 0))

    return pl.pallas_call(
        functools.partial(
            attend_back_kernel,
            piece_count=piece_count,
            head_width=head_width,
            first=first,
            sum_count=len(sums),
            after_count=len(after),
        ),
        out_shape=(
            back_shape,
            back_shape,
            jax.ShapeDtypeStruct(weight_shape, bf16 if last else f32),
            jax.ShapeDtypeStruct((2, 8, head_width), f32),
        ),
        grid_spec=pltpu.PrefetchScalarGridSpec(
            num_scalar_prefetch=1,
            grid=(seqs,),
            in_specs=[pl.BlockSpec((1, block, width), lambda i, _: (first + i, 0, 0))] * piece_count
            + [pl.BlockSpec(weight.shape, lambda i, _: (0, 0, 0))]
            + [heads_spec] * 3
            + [pieces_spec(place), pieces_spec(first)]
            + [pl.BlockSpec((1, 8, full_len), lambda i, _: (place + i, 0, 0))]
            + [pl.BlockSpec(memory_space=pltpu.VMEM)] * len(sums)
            + [pl.BlockSpec(memory_space=pl.ANY)] * len(after),
            out_specs=(
                back_spec,
                back_spec,
                pl.BlockSpec(weight_shape, lambda i, _: (0, 0)),
                pl.BlockSpec((2, 8, head_width), lambda i, _: (0, 0, 0)),
            ),
            scratch_shapes=[
                pltpu.VMEM((head_width, full_len), f32),
                pltpu.VMEM((full_len, head_width), bf16),
                pltpu.VMEM((full_len, head_width), bf16),
            ]
            + [pltpu.VMEM((head_width, full_len), bf16)] * 3
            + [pltpu.VMEM(weight_shape, f32)] * last,
        ),
        compiler_params=pltpu.CompilerParams(vmem_limit_bytes=60 * MIB),
        cost_estimate=cost(12),
        input_output_aliases={inputs_count - 2 + i: i for i in range(len(backs))},
        name="attend_back",
    )(info, *x_parts, weight, query, key, value, mixed, grad, mass, *sums, *after)


def gather_exchange(value, axis):
    count = lax.axis_size(axis)
    spread = jnp.broadcast_to(value[None], (count,) + value.shape)
    return lax.all_to_all(spread, axis, split_axis=0, concat_axis=0, tiled=True)


def gather_relative(value, axis, order):
    pieces = [(0, value)]
    for step in order:
        pieces = pieces + [(offset ^ step, xor_permute(piece, axis, step)) for offset, piece in pieces]
    return pieces


def gather_direct(value, axis):
    count = lax.axis_size(axis)
    return [value] + [xor_permute(value, axis, step) for step in range(1, count)]


def gather_batch(value):
    count = lax.axis_size("batch")
    pieces = []
    for step in range(0, count, 2):
        piece = xor_permute(value, "batch", step) if step else value
        pieces += [piece, xor_permute(piece, "batch", 1)]
    return pieces


def sum_upper(parts):
    total = parts[0]
    for step in range(1, len(parts)):
        total = total + xor_permute(parts[step], "batch", 2 * step).astype(f32)
    return total


def natural(pieces, index):
    return jnp.take(jnp.stack(pieces), index ^ jnp.arange(len(pieces)), axis=0)


def deal_gram(info, rows):
    keep, send = gram(info, rows)
    got = xor_permute(send, "seq", 1)
    return deal(lax.axis_index("batch"), keep, got, lax.axis_size("batch"))


def sum_gram(stay, leave):
    halves_sum = stay + xor_permute(leave, "batch", 1)
    own = sum_upper([halves_sum[k] for k in range(halves_sum.shape[0])])
    mine = gather_batch(own)
    return mine, [xor_permute(part, "seq", 1) for part in mine]


def shards(
    inputs,
    counts,
    cotangent,
    attention_weights,
    attention_momenta,
    feed_weights,
    feed_momenta,
    vector_params,
    vector_first,
    vector_second,
):
    seqs, local_len, width = inputs.shape
    seq_count, batch_count = lax.axis_size("seq"), lax.axis_size("batch")
    seq_index, batch_index = lax.axis_index("seq"), lax.axis_index("batch")
    full_len = local_len * seq_count
    tokens_count = seqs * local_len
    head_width = width // seq_count
    head_count = head_width // HEAD_DIM
    column_width = attention_weights.shape[2]
    feed_width = feed_weights.shape[2]
    hidden = feed_width * batch_count * seq_count
    vector_rows = vector_params.shape[0]

    att_own = attention_weights[0].T
    feed_own = feed_weights.transpose(0, 2, 1)
    moment_own = attention_momenta[0].T
    feed_moment_own = feed_momenta.transpose(0, 2, 1)
    vec_low = vector_params.astype(bf16)

    pad = jnp.zeros((16, width), bf16).at[0, : vector_rows * column_width].set(vec_low.reshape(-1))
    feed_payload = jnp.concatenate([feed_own.astype(bf16).reshape(-1, width), pad], axis=0)
    feed_all = lax.all_gather(feed_payload, ("seq", "batch"), axis=0, tiled=False)
    moment_all = lax.all_gather(moment_own, "batch", axis=0, tiled=True)
    x_parts = gather_relative(inputs, "seq", [2, 1])
    x_parts = [piece for _, piece in sorted(x_parts, key=lambda pair: pair[0])]
    payload = jnp.concatenate([att_own.astype(bf16), pad], axis=0)
    member_parts = gather_exchange(payload, "batch")
    member_vecs = member_parts[:, column_width, : vector_rows * column_width]
    member_vecs = member_vecs.reshape(batch_count, vector_rows, column_width)
    member_vecs = member_vecs.transpose(1, 0, 2).reshape(1, vector_rows, width)
    member_vecs = jnp.pad(member_vecs, ((0, 0), (0, 16 - vector_rows), (0, 0)))
    member_rows = member_parts[:, :column_width].reshape(seq_count, head_width, width)
    head_weights = lax.all_to_all(
        jnp.concatenate(
            [member_rows, jnp.broadcast_to(member_vecs, (seq_count, 16, width))], axis=1
        ),
        "seq",
        split_axis=0,
        concat_axis=0,
        tiled=True,
    )
    output_parts = gather_direct(head_weights[3, :head_width], "seq")
    vec_full = feed_all[:, 2 * feed_width, : vector_rows * column_width]
    vec_full = vec_full.reshape(seq_count, batch_count, vector_rows, column_width)
    vec_full = vec_full.transpose(0, 2, 1, 3).reshape(12, width).astype(f32)
    bias_up = vec_full[3:7].reshape(batch_count, seq_count, feed_width)
    bias_up = bias_up.transpose(1, 0, 2).reshape(hidden)

    upper = seq_count // 2
    matrix = seq_index // upper
    moment_send = lax.dynamic_index_in_dim(feed_moment_own, 1 - matrix, 0, keepdims=False)
    moment_keep = lax.dynamic_index_in_dim(feed_moment_own, matrix, 0, keepdims=False)
    moment_other = xor_permute(moment_send, "seq", upper)

    info = jnp.concatenate([seq_index.astype(jnp.int32)[None], counts])
    ranges = ((0, 1), (1, seqs - 1))
    saved, mixed_tok = [], []
    for turn, (first, count) in enumerate(ranges):
        saved.append(
            attend(info, x_parts, head_weights, first, count, output_parts[1:] if turn else ())
        )
        mixed_tok.append(
            lax.all_to_all(saved[-1][3], "seq", split_axis=0, concat_axis=0, tiled=True)
        )

    (
        grad_mixed,
        layer_out,
        gate,
        grad_up,
        normed,
        grad_down,
        grad_attn,
        mixed_flat,
        grad_rest,
        vec_sums,
        up_sums,
    ) = token_part(
        info, inputs, mixed_tok, cotangent, feed_all, vec_full, bias_up[None], output_parts, ranges
    )
    grad_heads = lax.all_to_all(grad_mixed, "seq", split_axis=0, concat_axis=0, tiled=True)
    pair_keep, pair_send, output_grads = weight_grads(
        info, gate, grad_up, normed, grad_down, grad_attn, mixed_flat, seq_count
    )
    output_got = [
        xor_permute(part, "seq", step) for step, part in enumerate(output_grads) if step
    ]

    pair_send, grad_heads = lax.optimization_barrier((pair_send, grad_heads))
    pair_got = xor_permute(pair_send, "seq", 1)
    low_batch = batch_index % 2
    blocks_shape = (2, 2, batch_count // 2, 2, feed_width, width)
    pair_sum = pair_keep.reshape(blocks_shape).astype(f32)
    pair_sum = pair_sum + pair_got.reshape(blocks_shape).astype(f32)

    def keep_and_send(total, index, axis):
        keep = lax.dynamic_index_in_dim(total, index, axis, keepdims=False)
        send = lax.dynamic_index_in_dim(total, 1 - index, axis, keepdims=False)
        return keep, send.astype(bf16)

    one_keep, one_send = keep_and_send(pair_sum[:, 0], matrix, 0)
    two_keep, two_send = keep_and_send(pair_sum[:, 1], low_batch, 2)
    sent = [(one_send, two_send)]
    one_got = xor_permute(one_send, "seq", upper)
    two_got = xor_permute(two_send, "batch", 1)

    before = ()
    for first in range(seqs):
        if first == 1:
            one_got, two_got, _ = lax.optimization_barrier((one_got, two_got, before[-1]))
            one_keep, one_send = keep_and_send(one_keep + one_got.astype(f32), low_batch, 1)
            two_keep, two_send = keep_and_send(two_keep + two_got.astype(f32), matrix, 0)
            sent.append((one_send, two_send))
            one_got = xor_permute(one_send, "batch", 1)
            two_got = xor_permute(two_send, "seq", upper)
        if first == 2:
            one_got, two_got, _ = lax.optimization_barrier((one_got, two_got, before[-1]))
            halves_sum = jnp.stack(
                [one_keep + one_got.astype(f32), two_keep + two_got.astype(f32)], axis=1
            ).astype(bf16)
            sent.append((halves_sum, moment_all))
        part = 0 if first < ranges[0][1] else 1
        before = attend_back(
            info,
            x_parts,
            head_weights,
            saved[part],
            grad_heads,
            first,
            first - ranges[part][0],
            before,
            sent[first],
            first == seqs - 1,
        )
        if first == 0:
            output_got, _ = lax.optimization_barrier((output_got, before[-1]))
    back_near, back_far, head_weight_grads, head_bias_grads = before
    back_got = xor_permute(back_far, "seq", 1)
    cross_send = (back_near[1].astype(f32) + back_got[1].astype(f32)).astype(bf16)

    feed_sum = lax.dynamic_index_in_dim(halves_sum, batch_index // 2, 0, keepdims=False)
    feed_sum = feed_sum.astype(f32)
    for step in range(1, batch_count // 2):
        part = lax.dynamic_index_in_dim(halves_sum, batch_index // 2 ^ step, 0, keepdims=False)
        feed_sum = feed_sum + xor_permute(part, "batch", 2 * step).astype(f32)
    mine_first = matrix == 0
    moment_pair = jnp.where(
        mine_first, jnp.stack([moment_keep, moment_other]), jnp.stack([moment_other, moment_keep])
    )
    feed_moment_pair = muon_decay * moment_pair + feed_sum
    feed_rows = feed_moment_pair.reshape(2 * feed_width, width)
    gram_stay, gram_leave = deal_gram(info, feed_rows)
    gram_mine, gram_other = sum_gram(gram_stay, gram_leave)
    output_sum = sum(part.astype(f32) for part in [output_grads[0], *output_got]).astype(bf16)
    att_grads = jnp.concatenate([head_weight_grads, output_sum])
    att_grads = att_grads.reshape(seq_count, batch_count, -1, width).transpose(1, 0, 2, 3)

    def at_heads(grad):
        own = jnp.arange(seq_count)[:, None] == seq_index
        return jnp.where(own, grad[0][None], 0.0).reshape(width)

    grad_bias_up = up_sums[0].reshape(seq_count, batch_count, feed_width)
    vec_grads = jnp.concatenate(
        [
            jnp.stack([at_heads(head_bias_grads[0]), at_heads(head_bias_grads[1]), vec_sums[0]]),
            grad_bias_up.transpose(1, 0, 2).reshape(4, width),
            vec_sums[1:6],
        ]
    )
    vec_grads = vec_grads.astype(bf16).reshape(seq_count, vector_rows, batch_count, column_width)
    vec_grads = vec_grads.transpose(2, 0, 1, 3).reshape(batch_count, seq_count, -1)
    att_rows = att_grads.shape[2]
    vec_grads = jnp.pad(vec_grads, ((0, 0), (0, 0), (0, att_rows * 128 - vec_grads.shape[2])))
    vec_grads = vec_grads.reshape(batch_count, seq_count, att_rows, 128)
    payload = jnp.concatenate([att_grads, vec_grads], axis=3)
    payload = payload.reshape(batch_count // 2, 2, seq_count, att_rows, width + 128)
    att_keep = lax.dynamic_index_in_dim(payload, low_batch, 1, keepdims=False)
    att_send = lax.dynamic_index_in_dim(payload, 1 - low_batch, 1, keepdims=False)
    att_got, _ = lax.optimization_barrier((xor_permute(att_send, "batch", 1), gram_leave))
    att_half = att_keep.astype(f32) + att_got.astype(f32)
    att_parts = [
        lax.dynamic_index_in_dim(att_half, (batch_index // 2) ^ step, 0, keepdims=False)
        for step in range(batch_count // 2)
    ]
    att_parts = [att_parts[0]] + [part.astype(bf16) for part in att_parts[1:]]
    att_total = sum_upper(att_parts).astype(bf16)
    att_got = lax.all_to_all(att_total, "seq", split_axis=0, concat_axis=0, tiled=True)
    att_sum = att_got[..., :width]
    cross_send, _ = lax.optimization_barrier((cross_send, att_got))
    cross_got = xor_permute(cross_send, "seq", upper)
    att_pieces = gather_batch(att_sum)
    grad_vec = jnp.sum(att_got[..., width:].astype(f32), axis=0).reshape(-1)
    grad_vec = grad_vec[: vector_rows * column_width].reshape(vector_rows, column_width)
    ortho_feed_pair = newton(
        batch_index, seq_index, gram_mine, gram_other, feed_rows, cross_got
    ).reshape(2, feed_width, width)
    grad_rest, cross_got, _ = lax.optimization_barrier((grad_rest, cross_got, ortho_feed_pair))
    grad_tokens = grad_rest.reshape(inputs.shape)
    back_sum = back_near[0].astype(f32) + back_got[0].astype(f32) + cross_got.astype(f32)
    input_grad = (grad_tokens + back_sum).astype(bf16)
    att_rows_own, ortho_att = newton_whole(
        batch_index, att_pieces, moment_all, column_width, ortho_feed_pair
    )
    feed_moment_pair, ortho_feed_pair = lax.optimization_barrier(
        (feed_moment_pair, ortho_feed_pair)
    )
    moment_keep = lax.dynamic_index_in_dim(feed_moment_pair, matrix, 0, keepdims=False)
    moment_send = lax.dynamic_index_in_dim(feed_moment_pair, 1 - matrix, 0, keepdims=False)
    moment_other = xor_permute(moment_send, "seq", upper)
    ortho_keep = lax.dynamic_index_in_dim(ortho_feed_pair, matrix, 0, keepdims=False)
    ortho_send = lax.dynamic_index_in_dim(ortho_feed_pair, 1 - matrix, 0, keepdims=False)
    ortho_other = xor_permute(ortho_send, "seq", upper)

    def by_matrix(keep, other):
        both = jnp.where(mine_first, jnp.stack([keep, other]), jnp.stack([other, keep]))
        return both.transpose(0, 2, 1)

    feed_moment = by_matrix(moment_keep, moment_other)
    ortho_feed = by_matrix(ortho_keep, ortho_other)

    attention_moment = att_rows_own.T[None]
    ortho_att = ortho_att.T[None]
    attention_next = attention_weights * (1.0 - muon_rate * decay_rate) - muon_rate * ortho_att
    feed_next = feed_weights * (1.0 - muon_rate * decay_rate) - muon_rate * ortho_feed
    vector_first_next = beta_one * vector_first + (1.0 - beta_one) * grad_vec
    vector_second_next = beta_two * vector_second + (1.0 - beta_two) * grad_vec * grad_vec
    first_hat = vector_first_next / (1.0 - beta_one**STEP)
    second_hat = vector_second_next / (1.0 - beta_two**STEP)
    vector_next = vector_params * (1.0 - adam_rate * decay_rate) - adam_rate * first_hat / (
        jnp.sqrt(second_hat) + adam_eps
    )
    return (
        layer_out,
        input_grad,
        attention_next,
        attention_moment,
        feed_next,
        feed_moment,
        vector_next,
        vector_first_next,
        vector_second_next,
    )


def solution(mesh):
    tokens_spec = P("batch", "seq", None)
    attention_spec = P("seq", None, "batch")
    feed_spec = P(None, None, ("batch", "seq"))
    vector_spec = P("seq", "batch")
    return jax.shard_map(
        shards,
        mesh=mesh,
        in_specs=(tokens_spec, P("batch"), tokens_spec)
        + (attention_spec,) * 2
        + (feed_spec,) * 2
        + (vector_spec,) * 3,
        out_specs=(tokens_spec,) * 2
        + (attention_spec,) * 2
        + (feed_spec,) * 2
        + (vector_spec,) * 3,
        check_vma=False,
    )
```

```python
import functools

import jax
import jax.numpy as jnp
from jax import lax
from jax.experimental import pallas as pl
from jax.experimental.pallas import tpu as pltpu
from jax.sharding import PartitionSpec as P

HEAD_DIM = 64
STEP = 10
NS_STEPS = 5

newton_coef = (3.4445, -4.775, 2.0315)
muon_rate = 0.6
muon_decay = 0.95
adam_rate = 0.3
beta_one = 0.9
beta_two = 0.999
decay_rate = 0.01
adam_eps = 1e-08
norm_eps = 1e-05
masked_score = -1e30
bf16 = jnp.bfloat16
f32 = jnp.float32
MIB = 1024 * 1024


def cost(micros):
    return pl.CostEstimate(flops=int(micros * 1.15e9), bytes_accessed=1 << 20, transcendentals=0)

NN = (((1,), (0,)), ((), ()))
NT = (((1,), (1,)), ((), ()))
TN = (((0,), (0,)), ((), ()))


def dot(left, right, dims=NN):
    return lax.dot_general(left, right, dims, preferred_element_type=f32)


def xor_permute(value, axis, step):
    count = lax.axis_size(axis)
    return lax.ppermute(value, axis, [(i, i ^ step) for i in range(count)])


def halves(value):
    high = value.astype(bf16)
    return high, (value - high.astype(f32)).astype(bf16)


def dot_split(left, right, dims=NN):
    (left_high, left_low), (right_high, right_low) = left, right
    return (
        dot(left_high, right_high, dims)
        + dot(left_high, right_low, dims)
        + dot(left_low, right_high, dims)
    )


def dot_split_wide(left, right):
    (left_high, left_low), (right_high, right_low) = left, right
    return dot(
        jnp.concatenate([left_high, left_high, left_low], axis=1),
        jnp.concatenate([right_high, right_low, right_high], axis=0),
    )


def newton_loop(square, rows):
    width = square.shape[0]
    for turn in range(NS_STEPS):
        square_parts, row_parts = halves(square), halves(rows)
        squared = dot_split_wide(square_parts, square_parts)
        poly_parts = halves(newton_coef[1] * square + newton_coef[2] * squared)
        if turn + 1 == NS_STEPS:
            return newton_coef[0] * rows + dot_split_wide(row_parts, poly_parts)
        both = [jnp.concatenate(pair, axis=0) for pair in zip(square_parts, row_parts)]
        made = dot_split_wide(both, poly_parts)
        rows = newton_coef[0] * rows + made[width:]
        once = newton_coef[0] * square + made[:width]
        square = newton_coef[0] * once + dot_split_wide(halves(once), poly_parts)


def gram_of_rows(rows):
    parts = halves(rows)
    return dot_split(parts, parts, TN)


def normalized(gram, rows):
    width = gram.shape[0]
    shape = (width, width)
    on_diagonal = lax.broadcasted_iota(jnp.int32, shape, 0) == lax.broadcasted_iota(
        jnp.int32, shape, 1
    )
    trace = jnp.sum(jnp.where(on_diagonal, gram, 0.0), keepdims=True)
    factor = 1.0 / (jnp.sqrt(trace) + 1e-07)
    return gram * (factor * factor), rows * factor


def gram_kernel(info_ref, rows_ref, *refs):
    total_ref = refs[2]
    total_ref[...] = gram_of_rows(rows_ref[...])
    for distance, out_ref in enumerate(refs[:2]):
        size = out_ref.shape[0]
        start = pl.multiple_of(((info_ref[0] % 2) ^ distance) * size, size)
        out_ref[...] = total_ref[pl.ds(start, size), :]


def gram(info, rows):
    width = rows.shape[1]
    half = jax.ShapeDtypeStruct((width // 2, width), f32)
    vmem = pl.BlockSpec(memory_space=pltpu.VMEM)
    return pl.pallas_call(
        gram_kernel,
        out_shape=(half, half),
        in_specs=[pl.BlockSpec(memory_space=pltpu.SMEM), vmem],
        out_specs=(vmem, vmem),
        scratch_shapes=[pltpu.VMEM((width, width), f32)],
        compiler_params=pltpu.CompilerParams(vmem_limit_bytes=10 * MIB),
        cost_estimate=cost(2),
        name="gram",
    )(info, rows)


def deal_kernel(index_ref, left_ref, right_ref, *out_refs):
    size = out_refs[0].shape[1]
    for side, out_ref in enumerate(out_refs):
        for distance in range(out_ref.shape[0]):
            block = index_ref[0] ^ (2 * distance + side)
            rows = pl.ds(pl.multiple_of(block * size, size), size)
            out_ref[distance] = left_ref[rows, :] + right_ref[rows, :]


def deal(index, left, right, count):
    rows = left.shape[0] // count
    if rows % 8:
        total = jnp.take((left + right).reshape(count, rows, -1), index ^ jnp.arange(count), axis=0)
        return total[0::2], total[1::2]
    vmem = pl.BlockSpec(memory_space=pltpu.VMEM)
    shape = jax.ShapeDtypeStruct((count // 2, rows, left.shape[1]), left.dtype)
    return pl.pallas_call(
        deal_kernel,
        out_shape=(shape, shape),
        in_specs=[pl.BlockSpec(memory_space=pltpu.SMEM), vmem, vmem],
        out_specs=(vmem, vmem),
        compiler_params=pltpu.CompilerParams(vmem_limit_bytes=6 * MIB),
        cost_estimate=cost(1),
        name="deal",
    )(index[None].astype(jnp.int32), left, right)


def newton_kernel(place_ref, *refs):
    rows_ref, _, out_ref, square_ref = refs[-4:]
    half = square_ref.shape[0] // 2
    parts = refs[:-4]
    for turn, part_ref in enumerate(parts):
        distance, side = turn % (len(parts) // 2), turn // (len(parts) // 2)
        size = part_ref.shape[0]
        place = (place_ref[0] ^ distance) * size if len(parts) > 2 else 0
        start = pl.multiple_of(((place_ref[1] % 2) ^ side) * half + place, 8)
        square_ref[pl.ds(start, size), :] = part_ref[...]
    out_ref[...] = newton_loop(*normalized(square_ref[...], rows_ref[...]))


def newton(batch_index, seq_index, mine, other, rows, after):
    width = rows.shape[1]
    if mine[0].shape[0] % 8:
        mine = [natural(mine, batch_index).reshape(-1, width)]
        other = [natural(other, batch_index).reshape(-1, width)]
    place = jnp.stack([batch_index, seq_index]).astype(jnp.int32)
    vmem = pl.BlockSpec(memory_space=pltpu.VMEM)
    return pl.pallas_call(
        newton_kernel,
        out_shape=jax.ShapeDtypeStruct(rows.shape, f32),
        in_specs=[pl.BlockSpec(memory_space=pltpu.SMEM)]
        + [vmem] * (len(mine) + len(other) + 1)
        + [pl.BlockSpec(memory_space=pl.ANY)],
        out_specs=vmem,
        scratch_shapes=[pltpu.VMEM((width, width), f32)],
        compiler_params=pltpu.CompilerParams(vmem_limit_bytes=20 * MIB),
        cost_estimate=cost(15),
        name="newton",
    )(place, *mine, *other, rows, after)


def newton_whole_kernel(index_ref, *refs, count):
    pieces, (old_ref, _, moment_ref, out_ref, rows_ref) = refs[:count], refs[count:]
    own = moment_ref.shape[0]
    members, step = pieces[0].shape[:2]
    stride = rows_ref.shape[0] // members
    for turn in range(count):
        place = (index_ref[0] ^ turn) * step if count > 1 else 0
        for member in range(members):
            rows = pl.ds(member * stride + pl.multiple_of(place, 8), step)
            rows_ref[rows, :] = muon_decay * old_ref[rows, :] + pieces[turn][member].astype(f32)
    gram = gram_of_rows(rows_ref[...])
    rows = rows_ref[pl.ds(pl.multiple_of(index_ref[0] * own, 8), own), :]
    moment_ref[...] = rows
    out_ref[...] = newton_loop(*normalized(gram, rows))


def newton_whole(index, pieces, old, own, after):
    if pieces[0].shape[1] % 8:
        pieces = [natural(pieces, index).transpose(1, 0, 2, 3).reshape(1, *old.shape)]
    shape = jax.ShapeDtypeStruct((own, old.shape[1]), f32)
    return pl.pallas_call(
        functools.partial(newton_whole_kernel, count=len(pieces)),
        out_shape=(shape, shape),
        in_specs=[pl.BlockSpec(memory_space=pltpu.SMEM)]
        + [pl.BlockSpec(memory_space=pltpu.VMEM)] * (len(pieces) + 1)
        + [pl.BlockSpec(memory_space=pl.ANY)],
        out_specs=(pl.BlockSpec(memory_space=pltpu.VMEM),) * 2,
        scratch_shapes=[pltpu.VMEM(old.shape, f32)],
        compiler_params=pltpu.CompilerParams(vmem_limit_bytes=22 * MIB),
        cost_estimate=cost(17),
        name="newton_whole",
    )(index[None].astype(jnp.int32), *pieces, old, after)


def norm_parts(values_in):
    centre = values_in - jnp.mean(values_in, axis=-1, keepdims=True)
    inverse_dev = lax.rsqrt(jnp.mean(centre * centre, axis=-1, keepdims=True) + norm_eps)
    return centre * inverse_dev, inverse_dev


def norm_back(grad, normal, inverse_dev, gain):
    scaled = grad * gain
    mean_scaled = jnp.mean(scaled, axis=-1, keepdims=True)
    mean_normal = jnp.mean(scaled * normal, axis=-1, keepdims=True)
    return inverse_dev * (scaled - mean_scaled - normal * mean_normal)


def column_sum(values_in):
    return jnp.sum(values_in.astype(f32), axis=0, keepdims=True)


def token_kernel(info_ref, x_ref, cotangent_ref, feed_ref, vec_ref, up_bias_ref, *refs, ranges):
    seqs, block, width = x_ref.shape
    mixed_refs, refs = refs[: len(ranges)], refs[len(ranges) :]
    seq_count = mixed_refs[0].shape[0]
    output_refs, refs = refs[:seq_count], refs[seq_count:]
    output_grad_refs, refs = refs[:seq_count], refs[seq_count:]
    grad_mixed_ref, out_ref, rest_ref, sums_ref, up_sums_ref, *pair_refs = refs[:7]
    w_output_ref, slope_ref, gate_ref, up_grad_ref, mixed_flat_ref = refs[7:]
    tokens = seqs * block
    head_width = width // seq_count
    pieces, feed_width = feed_ref.shape[0], (feed_ref.shape[1] - 16) // 2
    chunk_pieces = max(1, pieces // 4)
    chunk = chunk_pieces * feed_width
    chunks = pieces // chunk_pieces

    def weights(matrix, i):
        rows = slice(matrix * feed_width, (matrix + 1) * feed_width)
        return feed_ref[i * chunk_pieces : (i + 1) * chunk_pieces, rows].reshape(chunk, width)

    def vec(row):
        return vec_ref[row : row + 1]

    for offset in range(seq_count):
        start = pl.multiple_of((info_ref[0] ^ offset) * head_width, head_width)
        w_output_ref[pl.ds(start, head_width), :] = output_refs[offset][...]
    for place in range(seq_count):
        lanes = slice(place * head_width, (place + 1) * head_width)
        for mixed_ref, (first, count) in zip(mixed_refs, ranges):
            rows = slice(first * block, (first + count) * block)
            mixed_flat_ref[rows, lanes] = mixed_ref[place].reshape(count * block, head_width)
    x = x_ref[...].reshape(tokens, width).astype(f32)
    attn_out = dot(mixed_flat_ref[...], w_output_ref[...], NT) + vec(2)
    normal_first, inverse_first = norm_parts(x + attn_out)
    normed = normal_first * vec(8) + vec(9)
    normed_low = normed.astype(bf16)
    down_out = vec(7)
    curve, cubic = (2.0 / jnp.pi) ** 0.5, 0.044715
    for i in range(chunks):
        lanes = slice(i * chunk, (i + 1) * chunk)
        up = dot(normed_low, weights(0, i), NT) + up_bias_ref[:, lanes]
        square = up * up
        bend = jnp.tanh(up * (curve + (curve * cubic) * square))
        half = 0.5 + 0.5 * bend
        gate = (up * half).astype(bf16)
        gate_ref[lanes, :] = gate.T
        slope_ref[:, lanes] = half + (0.5 * up) * (1.0 - bend * bend) * (
            curve + (3.0 * curve * cubic) * square
        )
        down_out = down_out + dot(gate, weights(1, i))
    normal_second, inverse_second = norm_parts(x + normed + down_out)
    out = normal_second * vec(10) + vec(11)
    out_ref[...] = out.astype(bf16).reshape(out_ref.shape)
    grad_out = cotangent_ref[...].reshape(tokens, width).astype(f32)
    grad_sum = norm_back(grad_out, normal_second, inverse_second, vec(10))
    sums_ref[4:5] = column_sum(grad_out * normal_second)
    sums_ref[5:6] = column_sum(grad_out)
    grad_down_low = grad_sum.astype(bf16)
    sums_ref[1:2] = column_sum(grad_down_low)
    grad_normed = grad_sum
    for i in range(chunks):
        lanes = slice(i * chunk, (i + 1) * chunk)
        grad_up = dot(grad_down_low, weights(1, i), NT) * slope_ref[:, lanes]
        grad_up_low = grad_up.astype(bf16)
        up_grad_ref[lanes, :] = grad_up_low.T
        up_sums_ref[0:1, lanes] = column_sum(grad_up_low)
        grad_normed = grad_normed + dot(grad_up_low, weights(0, i))
    grad_first = norm_back(grad_normed, normal_first, inverse_first, vec(8))
    sums_ref[2:3] = column_sum(grad_normed * normal_first)
    sums_ref[3:4] = column_sum(grad_normed)
    grad_attn_low = grad_first.astype(bf16)
    sums_ref[0:1] = column_sum(grad_attn_low)
    rest_ref[...] = grad_sum + grad_first
    grad_mixed = dot(grad_attn_low, w_output_ref[...]).astype(bf16)
    for place in range(seq_count):
        lanes = slice(place * head_width, (place + 1) * head_width)
        grad_mixed_ref[place] = grad_mixed[:, lanes].reshape(seqs, block, head_width)

    grad_attn_t = grad_attn_low.T
    w_output_ref[...] = dot(grad_attn_t, mixed_flat_ref[...]).astype(bf16)
    for distance, grad_ref in enumerate(output_grad_refs):
        start = pl.multiple_of((info_ref[0] ^ distance) * head_width, head_width)
        grad_ref[...] = w_output_ref[pl.ds(start, head_width), :]
    upper, rows = pair_refs[0].shape[1:3]
    for distance, grad_ref in enumerate(pair_refs):
        for part in range(upper):
            start = (part * 2 + ((info_ref[0] % 2) ^ distance)) * rows
            span = pl.ds(pl.multiple_of(start, rows), rows)
            grad_ref[0, part] = dot(up_grad_ref[span, :], normed_low).astype(bf16)
            grad_ref[1, part] = dot(gate_ref[span, :], grad_down_low).astype(bf16)


def token_part(info, x, mixed, cotangent, feed_all, vec_full, up_bias, output_parts, ranges):
    seqs, block, width = x.shape
    tokens = seqs * block
    if (feed_all.shape[1] - 16) // 2 % 16:
        rows = (feed_all.shape[1] - 16) // 2
        parts = [feed_all[:, i * rows : (i + 1) * rows].reshape(-1, width) for i in range(2)]
        feed_all = jnp.concatenate(parts + [jnp.zeros((16, width), bf16)])[None]
    hidden, seq_count = up_bias.shape[1], len(output_parts)

    def shape(*dims, kind=bf16):
        return jax.ShapeDtypeStruct(dims, kind)

    vmem = pl.BlockSpec(memory_space=pltpu.VMEM)
    return pl.pallas_call(
        functools.partial(token_kernel, ranges=ranges),
        out_shape=(
            *(shape(width // seq_count, width) for _ in range(seq_count)),
            shape(seq_count, seqs, block, width // seq_count),
            shape(seqs, block, width),
            shape(tokens, width, kind=f32),
            shape(8, width, kind=f32),
            shape(8, hidden, kind=f32),
            *(shape(2, seq_count // 2, hidden // seq_count, width) for _ in range(2)),
        ),
        in_specs=[pl.BlockSpec(memory_space=pltpu.SMEM)] + [vmem] * (5 + len(mixed) + len(output_parts)),
        out_specs=(vmem,) * (7 + seq_count),
        scratch_shapes=[
            pltpu.VMEM((width, width), bf16),
            pltpu.VMEM((tokens, hidden), f32),
            pltpu.VMEM((hidden, tokens), bf16),
            pltpu.VMEM((hidden, tokens), bf16),
            pltpu.VMEM((tokens, width), bf16),
        ],
        compiler_params=pltpu.CompilerParams(vmem_limit_bytes=60 * MIB),
        cost_estimate=cost(17),
        name="token_part",
    )(info, x, cotangent, feed_all, vec_full, up_bias, *mixed, *output_parts)


def attend_kernel(info_ref, *refs, piece_count, head_width, first):
    x_refs, weight_ref = refs[:piece_count], refs[piece_count]
    query_ref, key_ref, value_ref, mixed_ref, mass_ref, query_t_ref, value_t_ref = refs[-7:]
    seq_index, length = info_ref[0], info_ref[1 + first + pl.program_id(0)]
    block = x_refs[0].shape[1]
    heads = head_width // HEAD_DIM
    value_rows = value_t_ref.shape[0] // heads
    own_lanes = pl.ds(pl.multiple_of(seq_index * head_width, head_width), head_width)
    vecs = weight_ref[0, head_width:, own_lanes].astype(f32)
    ones = jnp.ones((value_rows - HEAD_DIM, block), bf16)
    for offset in range(piece_count):
        rows = pl.ds(pl.multiple_of((seq_index ^ offset) * block, block), block)
        x = x_refs[offset][0]
        query = dot(x, weight_ref[0, :head_width], NT) + vecs[0:1]
        query = query.astype(bf16) * jnp.asarray(HEAD_DIM**-0.5, bf16)
        query_ref[0, rows, :] = query
        query_t_ref[:, rows] = query.T
        key_ref[0, rows, :] = dot(x, weight_ref[1, :head_width], NT).astype(bf16)
        value = (dot(x, weight_ref[2, :head_width], NT) + vecs[1:2]).astype(bf16)
        value_ref[0, rows, :] = value
        value_t = value.T
        for head in range(heads):
            start = head * value_rows
            value_t_ref[start : start + HEAD_DIM, rows] = value_t[
                head * HEAD_DIM : (head + 1) * HEAD_DIM
            ]
            value_t_ref[start + HEAD_DIM : start + value_rows, rows] = ones
    live_blocks = (length + block - 1) // block

    full_len = piece_count * block
    span = full_len

    def attend_blocks(count):
        for start in range(0, full_len, span):
            rows = slice(start, start + span)
            outs = []
            for head in range(heads):
                lanes = slice(head * HEAD_DIM, (head + 1) * HEAD_DIM)
                query_t = query_t_ref[lanes, rows]
                tiles = []
                top = None
                for i in range(count):
                    tile = dot(key_ref[0, i * block : (i + 1) * block, lanes], query_t)
                    if i == count - 1:
                        live = lax.broadcasted_iota(jnp.int32, tile.shape, 0) + i * block < length
                        tile = jnp.where(live, tile, masked_score)
                    tiles.append(tile)
                    tile_top = jnp.max(tile, axis=0, keepdims=True)
                    top = tile_top if top is None else jnp.maximum(top, tile_top)
                value_span = slice(head * value_rows, (head + 1) * value_rows)
                tiles = [jnp.exp(tile - top).astype(bf16) for tile in tiles]
                mixed = dot(
                    value_t_ref[value_span, : count * block], jnp.concatenate(tiles, axis=0)
                )
                mass = mixed[HEAD_DIM : HEAD_DIM + 1]
                outs.append(mixed[:HEAD_DIM] / mass)
                mass_ref[0, head : head + 1, rows] = top + jnp.log(mass)
            outs = jnp.concatenate(outs, axis=0).astype(bf16).T
            mixed_ref[start // block : (start + span) // block, 0] = outs.reshape(
                span // block, block, head_width
            )

    for count in range(1, piece_count + 1):
        pl.when(live_blocks == count)(functools.partial(attend_blocks, count))


def attend(info, x_parts, weight, first, seqs, after):
    piece_count = len(x_parts)
    _, block, width = x_parts[0].shape
    head_width = width // piece_count
    full_len = piece_count * block
    heads_shape = jax.ShapeDtypeStruct((seqs, full_len, head_width), bf16)
    heads_spec = pl.BlockSpec((1, full_len, head_width), lambda i, _: (i, 0, 0))
    return pl.pallas_call(
        functools.partial(
            attend_kernel, piece_count=piece_count, head_width=head_width, first=first
        ),
        out_shape=(heads_shape,) * 3
        + (
            jax.ShapeDtypeStruct((piece_count, seqs, block, head_width), bf16),
            jax.ShapeDtypeStruct((seqs, 8, full_len), f32),
        ),
        grid_spec=pltpu.PrefetchScalarGridSpec(
            num_scalar_prefetch=1,
            grid=(seqs,),
            in_specs=[pl.BlockSpec((1, block, width), lambda i, _: (first + i, 0, 0))] * piece_count
            + [pl.BlockSpec(weight.shape, lambda i, _: (0, 0, 0))]
            + [pl.BlockSpec(memory_space=pl.ANY)] * len(after),
            out_specs=(heads_spec,) * 3
            + (
                pl.BlockSpec((piece_count, 1, block, head_width), lambda i, _: (0, i, 0, 0)),
                pl.BlockSpec((1, 8, full_len), lambda i, _: (i, 0, 0)),
            ),
            scratch_shapes=[
                pltpu.VMEM((head_width, full_len), bf16),
                pltpu.VMEM((head_width // HEAD_DIM * (HEAD_DIM + 16), full_len), bf16),
            ],
        ),
        compiler_params=pltpu.CompilerParams(vmem_limit_bytes=60 * MIB),
        cost_estimate=cost(7 * seqs),
        name="attend",
    )(info, *x_parts, weight, *after)


def attend_back_kernel(info_ref, *refs, piece_count, head_width, first, sum_count, after_count):
    x_refs, refs = refs[:piece_count], refs[piece_count:]
    weight_ref, query_ref, key_ref, value_ref, mixed_ref, grad_ref, mass_ref = refs[:7]
    sum_refs, refs = refs[7 : 7 + sum_count], refs[7 + sum_count + after_count :]
    back_refs, weight_out_ref, bias_grad_ref, query_acc, key_acc, value_acc = refs[:2], *refs[2:7]
    query_t_ref, grad_t_ref, key_t_ref = refs[7:10]
    weight_grad_ref = refs[10] if refs[10:] else weight_out_ref
    step = pl.program_id(0)
    seq_index, length = info_ref[0], info_ref[1 + first + step]
    block = x_refs[0].shape[1]
    scale = HEAD_DIM**-0.5
    live_blocks = (length + block - 1) // block
    heads = head_width // HEAD_DIM
    query_acc[...] = jnp.zeros_like(query_acc)

    inner = []
    head_of_lane = lax.broadcasted_iota(jnp.int32, (8, head_width), 1) // HEAD_DIM
    picks = (head_of_lane == lax.broadcasted_iota(jnp.int32, (8, head_width), 0)).astype(bf16)
    for place in range(piece_count):
        columns = slice(place * block, (place + 1) * block)
        grad = grad_ref[place, 0]
        product = mixed_ref[place, 0].astype(f32) * grad.astype(f32)
        high, low = halves(product)
        inner.append(dot(picks, high, NT) + dot(picks, low, NT))
        query_t_ref[:, columns] = query_ref[0, columns, :].T
        key_t_ref[:, columns] = key_ref[0, columns, :].T
        grad_t_ref[:, columns] = grad.T

    inner = jnp.concatenate(inner, axis=1)
    full_len = piece_count * block
    span = full_len

    def key_block(k, masked):
        rows = pl.ds(pl.multiple_of(k * block, block), block)
        key_out, value_out = [], []
        for head in range(heads):
            lanes = slice(head * HEAD_DIM, (head + 1) * HEAD_DIM)
            key, value, key_t = key_ref[0, rows, lanes], value_ref[0, rows, lanes], key_t_ref[lanes, rows]
            key_grad, value_grad = None, None
            for start in range(0, full_len, span):
                columns = slice(start, start + span)
                tile = dot(key, query_t_ref[lanes, columns]) - mass_ref[0, head : head + 1, columns]
                if masked:
                    live = lax.broadcasted_iota(jnp.int32, tile.shape, 0) + k * block < length
                    tile = jnp.where(live, tile, masked_score)
                weights = jnp.exp(tile)
                tile = dot(value, grad_t_ref[lanes, columns]) - inner[head : head + 1, columns]
                score_grad = (weights * tile).astype(bf16)
                grad = grad_ref[start // block : (start + span) // block, 0, :, lanes]
                part = dot(weights.astype(bf16), grad.reshape(span, HEAD_DIM))
                value_grad = part if value_grad is None else value_grad + part
                part = dot(score_grad, query_ref[0, columns, lanes])
                key_grad = part if key_grad is None else key_grad + part
                query_acc[lanes, columns] += dot(key_t, score_grad)
            key_out.append(key_grad)
            value_out.append(value_grad)
        key_acc[rows, :] = jnp.concatenate(key_out, axis=1).astype(bf16)
        value_acc[rows, :] = jnp.concatenate(value_out, axis=1).astype(bf16)

    @pl.loop(0, live_blocks - 1)
    def _(k):
        key_block(k, False)

    key_block(live_blocks - 1, True)

    @pl.loop(live_blocks, piece_count)
    def _(k):
        rows = pl.ds(pl.multiple_of(k * block, block), block)
        key_acc[rows, :] = jnp.zeros((block, head_width), bf16)
        value_acc[rows, :] = jnp.zeros((block, head_width), bf16)

    @pl.when(step == 0)
    def _():
        if sum_refs:
            weight_grad_ref[...] = sum_refs[0][...]
            bias_grad_ref[...] = sum_refs[1][...]
        else:
            weight_grad_ref[...] = jnp.zeros_like(weight_grad_ref)
            bias_grad_ref[...] = jnp.zeros_like(bias_grad_ref)

    ones = jnp.ones((8, block), bf16)
    for offset in range(piece_count):
        start = pl.multiple_of((seq_index ^ offset) * block, block)
        rows = pl.ds(start, block)
        query_grad_t = (query_acc[:, rows] * scale).astype(bf16)
        query_grad = query_grad_t.T
        key_grad, value_grad = key_acc[rows, :], value_acc[rows, :]
        x = x_refs[offset][0]
        weight_grad_ref[:head_width] += dot(query_grad_t, x)
        weight_grad_ref[head_width : 2 * head_width] += dot(key_grad, x, TN)
        weight_grad_ref[2 * head_width :] += dot(value_grad, x, TN)
        bias_grad_ref[0] += dot(ones, query_grad)
        bias_grad_ref[1] += dot(ones, value_grad)
        back = dot(query_grad, weight_ref[0, :head_width])
        back = back + dot(key_grad, weight_ref[1, :head_width])
        back = back + dot(value_grad, weight_ref[2, :head_width])
        back_refs[offset % 2][offset // 2, 0] = back.astype(bf16)
    if weight_grad_ref is not weight_out_ref:
        weight_out_ref[...] = weight_grad_ref[...].astype(bf16)


def attend_back(info, x_parts, weight, saved, grad, first, place, before, after, last):
    piece_count = len(x_parts)
    _, block, width = x_parts[0].shape
    head_width = width // piece_count
    full_len = piece_count * block
    query, key, value, mixed, mass = saved
    seqs, all_seqs = 1, x_parts[0].shape[0]
    backs, sums = before[:2], before[2:]
    back_shape = jax.ShapeDtypeStruct((piece_count // 2, all_seqs, block, width), bf16)
    back_spec = pl.BlockSpec((piece_count // 2, 1, block, width), lambda i, _: (0, first + i, 0, 0))
    weight_shape = (3 * head_width, width)
    after = (*after, *backs)
    inputs_count = 1 + piece_count + 1 + 3 + 2 + 1 + len(sums) + len(after)
    heads_spec = pl.BlockSpec((1, full_len, head_width), lambda i, _: (place + i, 0, 0))

    def pieces_spec(row):
        return pl.BlockSpec((piece_count, 1, block, head_width), lambda i, _: (0, row + i, 0, 0))

    return pl.pallas_call(
        functools.partial(
            attend_back_kernel,
            piece_count=piece_count,
            head_width=head_width,
            first=first,
            sum_count=len(sums),
            after_count=len(after),
        ),
        out_shape=(
            back_shape,
            back_shape,
            jax.ShapeDtypeStruct(weight_shape, bf16 if last else f32),
            jax.ShapeDtypeStruct((2, 8, head_width), f32),
        ),
        grid_spec=pltpu.PrefetchScalarGridSpec(
            num_scalar_prefetch=1,
            grid=(seqs,),
            in_specs=[pl.BlockSpec((1, block, width), lambda i, _: (first + i, 0, 0))] * piece_count
            + [pl.BlockSpec(weight.shape, lambda i, _: (0, 0, 0))]
            + [heads_spec] * 3
            + [pieces_spec(place), pieces_spec(first)]
            + [pl.BlockSpec((1, 8, full_len), lambda i, _: (place + i, 0, 0))]
            + [pl.BlockSpec(memory_space=pltpu.VMEM)] * len(sums)
            + [pl.BlockSpec(memory_space=pl.ANY)] * len(after),
            out_specs=(
                back_spec,
                back_spec,
                pl.BlockSpec(weight_shape, lambda i, _: (0, 0)),
                pl.BlockSpec((2, 8, head_width), lambda i, _: (0, 0, 0)),
            ),
            scratch_shapes=[
                pltpu.VMEM((head_width, full_len), f32),
                pltpu.VMEM((full_len, head_width), bf16),
                pltpu.VMEM((full_len, head_width), bf16),
            ]
            + [pltpu.VMEM((head_width, full_len), bf16)] * 3
            + [pltpu.VMEM(weight_shape, f32)] * last,
        ),
        compiler_params=pltpu.CompilerParams(vmem_limit_bytes=60 * MIB),
        cost_estimate=cost(12),
        input_output_aliases={inputs_count - 2 + i: i for i in range(len(backs))},
        name="attend_back",
    )(info, *x_parts, weight, query, key, value, mixed, grad, mass, *sums, *after)


def gather_exchange(value, axis):
    count = lax.axis_size(axis)
    spread = jnp.broadcast_to(value[None], (count,) + value.shape)
    return lax.all_to_all(spread, axis, split_axis=0, concat_axis=0, tiled=True)


def gather_relative(value, axis, order):
    pieces = [(0, value)]
    for step in order:
        pieces = pieces + [(offset ^ step, xor_permute(piece, axis, step)) for offset, piece in pieces]
    return pieces


def gather_direct(value, axis):
    count = lax.axis_size(axis)
    return [value] + [xor_permute(value, axis, step) for step in range(1, count)]


def gather_batch(value):
    count = lax.axis_size("batch")
    pieces = []
    for step in range(0, count, 2):
        piece = xor_permute(value, "batch", step) if step else value
        pieces += [piece, xor_permute(piece, "batch", 1)]
    return pieces


def sum_upper(parts):
    total = parts[0]
    for step in range(1, len(parts)):
        total = total + xor_permute(parts[step], "batch", 2 * step).astype(f32)
    return total


def natural(pieces, index):
    return jnp.take(jnp.stack(pieces), index ^ jnp.arange(len(pieces)), axis=0)


def deal_gram(info, rows):
    keep, send = gram(info, rows)
    got = xor_permute(send, "seq", 1)
    return deal(lax.axis_index("batch"), keep, got, lax.axis_size("batch"))


def sum_gram(stay, leave):
    halves_sum = stay + xor_permute(leave, "batch", 1)
    own = sum_upper([halves_sum[k] for k in range(halves_sum.shape[0])])
    mine = gather_batch(own)
    return mine, [xor_permute(part, "seq", 1) for part in mine]


def shards(
    inputs,
    counts,
    cotangent,
    attention_weights,
    attention_momenta,
    feed_weights,
    feed_momenta,
    vector_params,
    vector_first,
    vector_second,
):
    seqs, local_len, width = inputs.shape
    seq_count, batch_count = lax.axis_size("seq"), lax.axis_size("batch")
    seq_index, batch_index = lax.axis_index("seq"), lax.axis_index("batch")
    full_len = local_len * seq_count
    tokens_count = seqs * local_len
    head_width = width // seq_count
    head_count = head_width // HEAD_DIM
    column_width = attention_weights.shape[2]
    feed_width = feed_weights.shape[2]
    hidden = feed_width * batch_count * seq_count
    vector_rows = vector_params.shape[0]

    att_own = attention_weights[0].T
    feed_own = feed_weights.transpose(0, 2, 1)
    moment_own = attention_momenta[0].T
    feed_moment_own = feed_momenta.transpose(0, 2, 1)
    vec_low = vector_params.astype(bf16)

    pad = jnp.zeros((16, width), bf16).at[0, : vector_rows * column_width].set(vec_low.reshape(-1))
    feed_payload = jnp.concatenate([feed_own.astype(bf16).reshape(-1, width), pad], axis=0)
    feed_all = lax.all_gather(feed_payload, ("seq", "batch"), axis=0, tiled=False)
    moment_all = lax.all_gather(moment_own, "batch", axis=0, tiled=True)
    x_parts = gather_relative(inputs, "seq", [2, 1])
    x_parts = [piece for _, piece in sorted(x_parts, key=lambda pair: pair[0])]
    payload = jnp.concatenate([att_own.astype(bf16), pad[:8]], axis=0)
    member_parts = gather_exchange(payload, "batch")
    member_vecs = member_parts[:, column_width, : vector_rows * column_width]
    member_vecs = member_vecs.reshape(batch_count, vector_rows, column_width)
    member_vecs = member_vecs.transpose(1, 0, 2).reshape(1, vector_rows, width)
    member_vecs = jnp.pad(member_vecs, ((0, 0), (0, 16 - vector_rows), (0, 0)))
    member_rows = member_parts[:, :column_width].reshape(seq_count, head_width, width)
    head_weights = lax.all_to_all(
        jnp.concatenate(
            [member_rows, jnp.broadcast_to(member_vecs, (seq_count, 16, width))], axis=1
        ),
        "seq",
        split_axis=0,
        concat_axis=0,
        tiled=True,
    )
    output_parts = gather_direct(head_weights[3, :head_width], "seq")
    vec_full = feed_all[:, 2 * feed_width, : vector_rows * column_width]
    vec_full = vec_full.reshape(seq_count, batch_count, vector_rows, column_width)
    vec_full = vec_full.transpose(0, 2, 1, 3).reshape(12, width).astype(f32)
    bias_up = vec_full[3:7].reshape(batch_count, seq_count, feed_width)
    bias_up = bias_up.transpose(1, 0, 2).reshape(hidden)

    upper = seq_count // 2
    matrix = seq_index // upper
    moment_send = lax.dynamic_index_in_dim(feed_moment_own, 1 - matrix, 0, keepdims=False)
    moment_keep = lax.dynamic_index_in_dim(feed_moment_own, matrix, 0, keepdims=False)
    moment_other = xor_permute(moment_send, "seq", upper)

    info = jnp.concatenate([seq_index.astype(jnp.int32)[None], counts])
    ranges = ((0, 1), (1, seqs - 1))
    saved, mixed_tok = [], []
    for turn, (first, count) in enumerate(ranges):
        saved.append(
            attend(info, x_parts, head_weights, first, count, output_parts[1:] if turn else ())
        )
        mixed_tok.append(
            lax.all_to_all(saved[-1][3], "seq", split_axis=0, concat_axis=0, tiled=True)
        )

    (
        *output_grads,
        grad_mixed,
        layer_out,
        grad_rest,
        vec_sums,
        up_sums,
        pair_keep,
        pair_send,
    ) = token_part(
        info, inputs, mixed_tok, cotangent, feed_all, vec_full, bias_up[None], output_parts, ranges
    )
    grad_heads = lax.all_to_all(grad_mixed, "seq", split_axis=0, concat_axis=0, tiled=True)
    output_got = [
        xor_permute(part, "seq", step) for step, part in enumerate(output_grads) if step
    ]

    pair_got = xor_permute(pair_send, "seq", 1)
    low_batch = batch_index % 2
    blocks_shape = (2, 2, batch_count // 2, 2, feed_width, width)
    pair_sum = pair_keep.reshape(blocks_shape).astype(f32)
    pair_sum = pair_sum + pair_got.reshape(blocks_shape).astype(f32)

    def keep_and_send(total, index, axis):
        keep = lax.dynamic_index_in_dim(total, index, axis, keepdims=False)
        send = lax.dynamic_index_in_dim(total, 1 - index, axis, keepdims=False)
        return keep, send.astype(bf16)

    one_keep, one_send = keep_and_send(pair_sum[:, 0], matrix, 0)
    two_keep, two_send = keep_and_send(pair_sum[:, 1], low_batch, 2)
    sent = [(one_send, two_send)]
    one_got = xor_permute(one_send, "seq", upper)
    two_got = xor_permute(two_send, "batch", 1)

    before = ()
    for first in range(seqs):
        if first == 1:
            one_got, two_got, _ = lax.optimization_barrier((one_got, two_got, before[-1]))
            one_keep, one_send = keep_and_send(one_keep + one_got.astype(f32), low_batch, 1)
            two_keep, two_send = keep_and_send(two_keep + two_got.astype(f32), matrix, 0)
            sent.append((one_send, two_send))
            one_got = xor_permute(one_send, "batch", 1)
            two_got = xor_permute(two_send, "seq", upper)
        if first == 2:
            one_got, two_got, _ = lax.optimization_barrier((one_got, two_got, before[-1]))
            halves_sum = jnp.stack(
                [one_keep + one_got.astype(f32), two_keep + two_got.astype(f32)], axis=1
            ).astype(bf16)
            sent.append((halves_sum, moment_all))
        part = 0 if first < ranges[0][1] else 1
        before = attend_back(
            info,
            x_parts,
            head_weights,
            saved[part],
            grad_heads,
            first,
            first - ranges[part][0],
            before,
            sent[first],
            first == seqs - 1,
        )
        if first == 0:
            output_got, _ = lax.optimization_barrier((output_got, before[-1]))
    back_near, back_far, head_weight_grads, head_bias_grads = before
    back_got = xor_permute(back_far, "seq", 1)
    cross_send = (back_near[1].astype(f32) + back_got[1].astype(f32)).astype(bf16)

    feed_sum = lax.dynamic_index_in_dim(halves_sum, batch_index // 2, 0, keepdims=False)
    feed_sum = feed_sum.astype(f32)
    for step in range(1, batch_count // 2):
        part = lax.dynamic_index_in_dim(halves_sum, batch_index // 2 ^ step, 0, keepdims=False)
        feed_sum = feed_sum + xor_permute(part, "batch", 2 * step).astype(f32)
    mine_first = matrix == 0
    moment_pair = jnp.where(
        mine_first, jnp.stack([moment_keep, moment_other]), jnp.stack([moment_other, moment_keep])
    )
    feed_moment_pair = muon_decay * moment_pair + feed_sum
    feed_rows = feed_moment_pair.reshape(2 * feed_width, width)
    gram_stay, gram_leave = deal_gram(info, feed_rows)
    gram_mine, gram_other = sum_gram(gram_stay, gram_leave)
    output_sum = sum(part.astype(f32) for part in [output_grads[0], *output_got]).astype(bf16)
    att_grads = jnp.concatenate([head_weight_grads, output_sum])
    att_grads = att_grads.reshape(seq_count, batch_count, -1, width).transpose(1, 0, 2, 3)

    def at_heads(grad):
        own = jnp.arange(seq_count)[:, None] == seq_index
        return jnp.where(own, grad[0][None], 0.0).reshape(width)

    grad_bias_up = up_sums[0].reshape(seq_count, batch_count, feed_width)
    vec_grads = jnp.concatenate(
        [
            jnp.stack([at_heads(head_bias_grads[0]), at_heads(head_bias_grads[1]), vec_sums[0]]),
            grad_bias_up.transpose(1, 0, 2).reshape(4, width),
            vec_sums[1:6],
        ]
    )
    vec_grads = vec_grads.astype(bf16).reshape(seq_count, vector_rows, batch_count, column_width)
    vec_grads = vec_grads.transpose(2, 0, 1, 3).reshape(batch_count, seq_count, -1)
    att_rows = att_grads.shape[2]
    vec_grads = jnp.pad(vec_grads, ((0, 0), (0, 0), (0, att_rows * 128 - vec_grads.shape[2])))
    vec_grads = vec_grads.reshape(batch_count, seq_count, att_rows, 128)
    payload = jnp.concatenate([att_grads, vec_grads], axis=3)
    payload = payload.reshape(batch_count // 2, 2, seq_count, att_rows, width + 128)
    att_keep = lax.dynamic_index_in_dim(payload, low_batch, 1, keepdims=False)
    att_send = lax.dynamic_index_in_dim(payload, 1 - low_batch, 1, keepdims=False)
    att_got, _ = lax.optimization_barrier((xor_permute(att_send, "batch", 1), gram_leave))
    att_half = att_keep.astype(f32) + att_got.astype(f32)
    att_parts = [
        lax.dynamic_index_in_dim(att_half, (batch_index // 2) ^ step, 0, keepdims=False)
        for step in range(batch_count // 2)
    ]
    att_parts = [att_parts[0]] + [part.astype(bf16) for part in att_parts[1:]]
    att_total = sum_upper(att_parts).astype(bf16)
    att_got = lax.all_to_all(att_total, "seq", split_axis=0, concat_axis=0, tiled=True)
    att_sum = att_got[..., :width]
    cross_send, _ = lax.optimization_barrier((cross_send, att_got))
    cross_got = xor_permute(cross_send, "seq", upper)
    att_pieces = gather_batch(att_sum)
    grad_vec = jnp.sum(att_got[..., width:].astype(f32), axis=0).reshape(-1)
    grad_vec = grad_vec[: vector_rows * column_width].reshape(vector_rows, column_width)
    ortho_feed_pair = newton(
        batch_index, seq_index, gram_mine, gram_other, feed_rows, cross_got
    ).reshape(2, feed_width, width)
    grad_rest, cross_got, _ = lax.optimization_barrier((grad_rest, cross_got, ortho_feed_pair))
    grad_tokens = grad_rest.reshape(inputs.shape)
    back_sum = back_near[0].astype(f32) + back_got[0].astype(f32) + cross_got.astype(f32)
    input_grad = (grad_tokens + back_sum).astype(bf16)
    att_rows_own, ortho_att = newton_whole(
        batch_index, att_pieces, moment_all, column_width, ortho_feed_pair
    )
    feed_moment_pair, ortho_feed_pair = lax.optimization_barrier(
        (feed_moment_pair, ortho_feed_pair)
    )
    moment_keep = lax.dynamic_index_in_dim(feed_moment_pair, matrix, 0, keepdims=False)
    moment_send = lax.dynamic_index_in_dim(feed_moment_pair, 1 - matrix, 0, keepdims=False)
    moment_other = xor_permute(moment_send, "seq", upper)
    ortho_keep = lax.dynamic_index_in_dim(ortho_feed_pair, matrix, 0, keepdims=False)
    ortho_send = lax.dynamic_index_in_dim(ortho_feed_pair, 1 - matrix, 0, keepdims=False)
    ortho_other = xor_permute(ortho_send, "seq", upper)

    def by_matrix(keep, other):
        both = jnp.where(mine_first, jnp.stack([keep, other]), jnp.stack([other, keep]))
        return both.transpose(0, 2, 1)

    feed_moment = by_matrix(moment_keep, moment_other)
    ortho_feed = by_matrix(ortho_keep, ortho_other)

    attention_moment = att_rows_own.T[None]
    ortho_att = ortho_att.T[None]
    attention_next = attention_weights * (1.0 - muon_rate * decay_rate) - muon_rate * ortho_att
    feed_next = feed_weights * (1.0 - muon_rate * decay_rate) - muon_rate * ortho_feed
    vector_first_next = beta_one * vector_first + (1.0 - beta_one) * grad_vec
    vector_second_next = beta_two * vector_second + (1.0 - beta_two) * grad_vec * grad_vec
    first_hat = vector_first_next / (1.0 - beta_one**STEP)
    second_hat = vector_second_next / (1.0 - beta_two**STEP)
    vector_next = vector_params * (1.0 - adam_rate * decay_rate) - adam_rate * first_hat / (
        jnp.sqrt(second_hat) + adam_eps
    )
    return (
        layer_out,
        input_grad,
        attention_next,
        attention_moment,
        feed_next,
        feed_moment,
        vector_next,
        vector_first_next,
        vector_second_next,
    )


def solution(mesh):
    tokens_spec = P("batch", "seq", None)
    attention_spec = P("seq", None, "batch")
    feed_spec = P(None, None, ("batch", "seq"))
    vector_spec = P("seq", "batch")
    return jax.shard_map(
        shards,
        mesh=mesh,
        in_specs=(tokens_spec, P("batch"), tokens_spec)
        + (attention_spec,) * 2
        + (feed_spec,) * 2
        + (vector_spec,) * 3,
        out_specs=(tokens_spec,) * 2
        + (attention_spec,) * 2
        + (feed_spec,) * 2
        + (vector_spec,) * 3,
        check_vma=False,
    )
```
